32 devices in a mesh: segment: 4 (over z), space: 8 (over y, x, core).
Axes of the slice: x: 2, y: 2, z: 4, core: 2. Of those that a mesh axis runs over, the one named last changes fastest.
Arguments:
- video: bfloat16 [4, 2, 32, 24, 256], P(None, None, 'space'), may hold values from -6 to 6
- spatial_weight: bfloat16 [4, 2, 2, 2304, 256], P('segment'), may hold values from -0.125 to 0.125
- temporal_weight: bfloat16 [4, 2, 2, 768, 256], P('segment'), may hold values from -0.21875 to 0.21875
- section_blocks: int32 [4], P('segment'), may hold values from 1 to 2, as said below
Outputs:
- section_out: bfloat16 [4, 4, 2, 32, 24, 256], P('segment', None, None, 'space')
The draws below stay inside these ranges and needn't reach their ends.
Inputs may be any that keep to these rules, and one draw needn't show every extreme that they name: `section_blocks`: some section runs 2 blocks.
All inputs are finite; a program needn't handle non-finite values.
Results may differ from the reference program's by a relative error of at most 0.038.
Values may be sent and summed in bfloat16 or wider, within the bound.
A program may use at most 64 MiB of HBM per device.

```python
import jax
import jax.numpy as jnp

C = 256
BLOCKS_MAX = 2
FRAMES = 2
COLS = 24
MICRO = 4
SEGMENTS = 4
ROWS = 32


def draw_section_blocks(key, part):
    first_key, second_key = jax.random.split(jax.random.fold_in(key, 11))
    counts = jax.random.randint(first_key, (SEGMENTS,), 1, BLOCKS_MAX + 1)
    chosen = jax.random.randint(second_key, (), 0, SEGMENTS)
    return counts.at[chosen].set(BLOCKS_MAX).astype(jnp.int32)


def levels(stream_key, extent, cuts, smallest, high):
    def one(position, parts):
        draws = jax.random.uniform(jax.random.fold_in(jax.random.fold_in(stream_key, 6), position), (parts,), jnp.float32, smallest / len(cuts), high / len(cuts))
        return jnp.repeat(jnp.exp(draws), extent[position] // parts).reshape((-1,) + (1,) * (len(extent) - position - 1))

    level = one(*cuts[0])
    for cut in cuts[1:]:
        level = level * one(*cut)
    return level


def centred(rng, extent, scale, limit, cuts=(), dtype=jnp.bfloat16):
    drawn = scale * jax.random.normal(rng, extent, jnp.float32)
    if cuts:
        drawn = drawn * levels(rng, extent, cuts, -0.22, 0.18)
    return jnp.clip(drawn, -limit, limit).astype(dtype)


def setup_inputs(seed: int = 0) -> dict:
    key_list = jax.random.split(jax.random.key(seed), 5)
    return {
        "video": centred(key_list[0], (MICRO, FRAMES, ROWS, COLS, C), 1.0, 6.0, ((2, 8),)),
        "spatial_weight": centred(key_list[1], (SEGMENTS, BLOCKS_MAX, 2, 9 * C, C), (9 * C) ** -0.5, 0.125, ((0, 4),)),
        "temporal_weight": centred(key_list[2], (SEGMENTS, BLOCKS_MAX, 2, 3 * C, C), (3 * C) ** -0.5, 0.21875, ((0, 4),)),
        "section_blocks": draw_section_blocks(jax.random.fold_in(key_list[4], 71), 0),
    }


def spatial_conv(active, weight):
    rows = active.shape[1]
    columns = active.shape[2]
    channels = active.shape[3]
    padded = jnp.pad(active, ((0, 0), (1, 1), (1, 1), (0, 0)))
    pieces = [padded[:, row_tap:row_tap + rows, col_tap:col_tap + columns] for row_tap in range(3) for col_tap in range(3)]
    stacked = jnp.concatenate(pieces, -1)
    summed = jnp.dot(stacked.reshape(-1, 9 * channels), weight, preferred_element_type=jnp.float32)
    return summed.reshape(active.shape)


def temporal_conv(stream, weight):
    frames = stream.shape[0]
    channels = stream.shape[3]
    joined = jnp.concatenate([stream[:1], stream[:1], stream], 0)
    stacked = jnp.concatenate([joined[0:frames], joined[1:frames + 1], joined[2:frames + 2]], -1)
    summed = jnp.dot(stacked.reshape(-1, 3 * channels), weight, preferred_element_type=jnp.float32)
    return summed.reshape(stream.shape)


def residual_block(state, ws_one, wt_one, ws_two, wt_two):
    active = jax.nn.silu(state.astype(jnp.float32)).astype(jnp.bfloat16)
    first_out = spatial_conv(active, ws_one).astype(jnp.bfloat16)
    hidden = jax.nn.silu(temporal_conv(first_out, wt_one)).astype(jnp.bfloat16)
    second_out = spatial_conv(hidden, ws_two).astype(jnp.bfloat16)
    return (state.astype(jnp.float32) + temporal_conv(second_out, wt_two)).astype(jnp.bfloat16)


def reference(video, spatial_weight, temporal_weight, section_blocks):
    state = video.reshape(MICRO * FRAMES, ROWS, COLS, C)
    results = []
    for section in range(SEGMENTS):
        for block in range(BLOCKS_MAX):
            updated = residual_block(state, spatial_weight[section, block, 0], temporal_weight[section, block, 0], spatial_weight[section, block, 1], temporal_weight[section, block, 1])
            state = jnp.where(block < section_blocks[section], updated, state)
        results.append(state.reshape(MICRO, FRAMES, ROWS, COLS, C))
    return jnp.stack(results)
```

```python
import functools

import jax
import jax.numpy as jnp
from jax import lax
from jax.experimental import pallas as pl
from jax.experimental.pallas import tpu as pltpu
from jax.sharding import PartitionSpec as P

MESH = pl.DeviceIdType.MESH


def silu(v):
    half = 0.5 * v
    return half + half * jnp.tanh(half)


def edge_rows(v, width, low_ok, high_ok):
    low = jnp.where(low_ok, v[:width], 0.0)
    high = jnp.where(high_ok, v[-width:], 0.0)
    return jnp.concatenate([low, v[width:-width], high], 0)


def kernel(
    segments, spaces, rows, cols,
    depth_ref, video_ref, ws_hbm, wt_hbm, out_ref,
    own, left, right, ws, wt, even, odd, caches,
    w_sem, z_send, z_recv, l_send, l_recv, r_send, r_recv,
):
    frames, cells, channels = video_ref.shape
    place = lax.axis_index("segment")
    spot = lax.axis_index("space")
    has_left = spot > 0
    has_right = spot < spaces - 1
    has_prev = place > 0
    has_next = place < segments - 1

    def w_copies(i):
        return (
            pltpu.make_async_copy(ws_hbm.at[i], ws.at[i], w_sem.at[2 * i]),
            pltpu.make_async_copy(wt_hbm.at[i], wt.at[i], w_sem.at[2 * i + 1]),
        )

    for i in range(4):
        for c in w_copies(i):
            c.start()

    to_next = {"segment": place + 1}
    to_prev = {"segment": place - 1}
    to_left = {"space": spot - 1}
    to_right = {"space": spot + 1}
    partners = ((has_prev, to_prev), (has_next, to_next), (has_left, to_left), (has_right, to_right))

    barrier = pltpu.get_barrier_semaphore()
    for there, target in partners:
        @pl.when(there)
        def _():
            pl.semaphore_signal(barrier, inc=1, device_id=target, device_id_type=MESH)

    @pl.when(place == 0)
    def _():
        own[...] = video_ref[...]

    @pl.when(spot == 0)
    def _():
        left[...] = jnp.zeros_like(left)

    @pl.when(spot == spaces - 1)
    def _():
        right[...] = jnp.zeros_like(right)

    peers = sum(there.astype(jnp.int32) for there, _target in partners)
    pl.semaphore_wait(barrier, peers)

    def z_copy(f):
        return pltpu.make_async_remote_copy(
            out_ref.at[f], own.at[f], z_send.at[f], z_recv.at[f],
            device_id=to_next, device_id_type=MESH,
        )

    def l_copy(f):
        return pltpu.make_async_remote_copy(
            own.at[f], right.at[f], l_send.at[f], l_recv.at[f],
            device_id=to_left, device_id_type=MESH,
        )

    def r_copy(f):
        return pltpu.make_async_remote_copy(
            own.at[f], left.at[f], r_send.at[f], r_recv.at[f],
            device_id=to_right, device_id_type=MESH,
        )

    def forward(f):
        @pl.when(has_prev)
        def _():
            z_copy(f).wait_recv()

        @pl.when(has_left)
        def _():
            l_copy(f).start()

        @pl.when(has_right)
        def _():
            r_copy(f).start()

    def spread(v, stage):
        count = v.shape[0] // cols
        grid = v.reshape(count, cols, channels)
        column = lax.broadcasted_iota(jnp.int32, grid.shape, 1)
        before = pltpu.roll(v, 1, 0).reshape(grid.shape)
        after = pltpu.roll(v, v.shape[0] - 1, 0).reshape(grid.shape)
        taps = (
            jnp.where(column == 0, 0.0, before).reshape(v.shape),
            v,
            jnp.where(column == cols - 1, 0.0, after).reshape(v.shape),
        )
        inner = v.shape[0] - 2 * cols
        for c, tap in enumerate(taps):
            even[stage][c] = tap.astype(jnp.bfloat16)
            odd[stage][c] = tap[cols:cols + inner].astype(jnp.bfloat16)

    def spatial(stage):
        size = odd[stage].shape[1]
        pieces = (
            [even[stage][c, 0:size] for c in range(3)]
            + [odd[stage][c] for c in range(3)]
            + [even[stage][c, 2 * cols:2 * cols + size] for c in range(3)]
        )
        lhs = jnp.concatenate(pieces, -1)
        return jnp.dot(lhs, ws[stage], preferred_element_type=jnp.float32)

    def conv(f, stage):
        @pl.when(f == 0)
        def _():
            w_copies(stage)[0].wait()

        first = spatial(stage).astype(jnp.bfloat16)
        cache = caches[stage]
        cache[lax.rem(f, 3)] = first

        @pl.when(f == 0)
        def _():
            w_copies(stage)[1].wait()
            cache[1] = first
            cache[2] = first

        lhs = jnp.concatenate([cache[lax.rem(f + 1, 3)], cache[lax.rem(f + 2, 3)], first], -1)
        return jnp.dot(lhs, wt[stage], preferred_element_type=jnp.float32)

    deep = depth_ref[0] > 1
    forward(0)

    def tick(f, carry):
        @pl.when(has_left)
        def _():
            r_copy(f).wait_recv()

        @pl.when(has_right)
        def _():
            l_copy(f).wait_recv()

        x = jnp.concatenate([left[f], own[f], right[f]], 0).astype(jnp.float32)
        spread(silu(x), 0)
        b = edge_rows(silu(conv(f, 0)), 3 * cols, has_left, has_right)

        @pl.when(f + 1 < frames)
        def _():
            forward(f + 1)

        spread(b, 1)
        x1 = (x[2 * cols:-2 * cols] + conv(f, 1)).astype(jnp.bfloat16).astype(jnp.float32)
        x1 = edge_rows(x1, 2 * cols, has_left, has_right)
        spread(silu(x1), 2)
        b = edge_rows(silu(conv(f, 2)), cols, has_left, has_right)
        spread(b, 3)
        mid = x1[2 * cols:-2 * cols]
        x2 = mid + conv(f, 3)
        out_ref[f] = jnp.where(deep, x2, mid).astype(jnp.bfloat16)

        @pl.when(has_next)
        def _():
            z_copy(f).start()

        return carry

    lax.fori_loop(0, frames, tick, 0)

    def drain(f, carry):
        @pl.when(has_next)
        def _():
            z_copy(f).wait_send()

        @pl.when(has_left)
        def _():
            l_copy(f).wait_send()

        @pl.when(has_right)
        def _():
            r_copy(f).wait_send()

        return carry

    lax.fori_loop(0, frames, drain, 0)


def per_device(segments, spaces, video, spatial_weight, temporal_weight, section_blocks):
    micro, frames, rows, cols, channels = video.shape
    steps = micro * frames
    cells = rows * cols
    spatial_set = spatial_weight.reshape(4, 9 * channels, channels)
    temporal_set = temporal_weight.reshape(4, 3 * channels, channels)
    bf16 = jnp.bfloat16
    sizes = [(3 * rows - 2 * i) * cols for i in range(5)]
    dma = pltpu.SemaphoreType.DMA
    out = pl.pallas_call(
        functools.partial(kernel, segments, spaces, rows, cols),
        out_shape=jax.ShapeDtypeStruct((steps, cells, channels), bf16),
        in_specs=[
            pl.BlockSpec(memory_space=pltpu.SMEM),
            pl.BlockSpec(memory_space=pltpu.VMEM),
            pl.BlockSpec(memory_space=pl.ANY),
            pl.BlockSpec(memory_space=pl.ANY),
        ],
        out_specs=pl.BlockSpec(memory_space=pltpu.VMEM),
        scratch_shapes=[
            pltpu.VMEM((steps, cells, channels), bf16),
            pltpu.VMEM((steps, cells, channels), bf16),
            pltpu.VMEM((steps, cells, channels), bf16),
            pltpu.VMEM(spatial_set.shape, bf16),
            pltpu.VMEM(temporal_set.shape, bf16),
            [pltpu.VMEM((3, sizes[i], channels), bf16) for i in range(4)],
            [pltpu.VMEM((3, sizes[i + 1], channels), bf16) for i in range(4)],
            [pltpu.VMEM((3, sizes[i + 1], channels), bf16) for i in range(4)],
            dma((8,)),
            dma((steps,)), dma((steps,)), dma((steps,)),
            dma((steps,)), dma((steps,)), dma((steps,)),
        ],
        compiler_params=pltpu.CompilerParams(
            collective_id=0, has_side_effects=True, vmem_limit_bytes=48 * 2**20
        ),
        name="sections",
    )(section_blocks, video.reshape(steps, cells, channels), spatial_set, temporal_set)
    return out.reshape(1, micro, frames, rows, cols, channels)


def solution(mesh):
    return jax.shard_map(
        functools.partial(per_device, mesh.shape["segment"], mesh.shape["space"]),
        mesh=mesh,
        in_specs=(
            P(None, None, "space", None, None),
            P("segment", None, None, None, None),
            P("segment", None, None, None, None),
            P("segment"),
        ),
        out_specs=P("segment", None, None, "space", None, None),
        check_vma=False,
    )
```

```python
import functools

import jax
import jax.numpy as jnp
from jax import lax
from jax.experimental import pallas as pl
from jax.experimental.pallas import tpu as pltpu
from jax.sharding import PartitionSpec as P

MESH = pl.DeviceIdType.MESH


def silu(v):
    half = 0.5 * v
    return half + half * jnp.tanh(half)


def edge_rows(v, width, low_ok, high_ok):
    low = jnp.where(low_ok, v[:width], 0.0)
    high = jnp.where(high_ok, v[-width:], 0.0)
    return jnp.concatenate([low, v[width:-width], high], 0)


def kernel(
    segments, spaces, rows, cols,
    depth_ref, video_ref, ws_hbm, wt_hbm, out_ref,
    own, left, right, ws, wt, even, odd, caches,
    w_sem, z_send, z_recv, l_send, l_recv, r_send, r_recv,
):
    frames, cells, channels = video_ref.shape
    place = lax.axis_index("segment")
    spot = lax.axis_index("space")
    has_left = spot > 0
    has_right = spot < spaces - 1
    has_prev = place > 0
    has_next = place < segments - 1

    def w_copies(i):
        return (
            pltpu.make_async_copy(ws_hbm.at[i], ws.at[i], w_sem.at[2 * i]),
            pltpu.make_async_copy(wt_hbm.at[i], wt.at[i], w_sem.at[2 * i + 1]),
        )

    for i in range(4):
        for c in w_copies(i):
            c.start()

    to_next = {"segment": place + 1}
    to_prev = {"segment": place - 1}
    to_left = {"space": spot - 1}
    to_right = {"space": spot + 1}
    partners = ((has_prev, to_prev), (has_next, to_next), (has_left, to_left), (has_right, to_right))

    barrier = pltpu.get_barrier_semaphore()
    for there, target in partners:
        @pl.when(there)
        def _():
            pl.semaphore_signal(barrier, inc=1, device_id=target, device_id_type=MESH)

    @pl.when(place == 0)
    def _():
        own[...] = video_ref[...]

    @pl.when(spot == 0)
    def _():
        left[...] = jnp.zeros_like(left)

    @pl.when(spot == spaces - 1)
    def _():
        right[...] = jnp.zeros_like(right)

    peers = sum(there.astype(jnp.int32) for there, _target in partners)
    pl.semaphore_wait(barrier, peers)

    def z_copy(f):
        return pltpu.make_async_remote_copy(
            out_ref.at[f], own.at[f], z_send.at[f], z_recv.at[f],
            device_id=to_next, device_id_type=MESH,
        )

    def l_copy(f):
        return pltpu.make_async_remote_copy(
            own.at[f], right.at[f], l_send.at[f], l_recv.at[f],
            device_id=to_left, device_id_type=MESH,
        )

    def r_copy(f):
        return pltpu.make_async_remote_copy(
            own.at[f], left.at[f], r_send.at[f], r_recv.at[f],
            device_id=to_right, device_id_type=MESH,
        )

    def forward(f):
        @pl.when(has_prev)
        def _():
            z_copy(f).wait_recv()

        @pl.when(has_left)
        def _():
            l_copy(f).start()

        @pl.when(has_right)
        def _():
            r_copy(f).start()

    def spread(v, stage):
        count = v.shape[0] // cols
        grid = v.reshape(count, cols, channels)
        column = lax.broadcasted_iota(jnp.int32, grid.shape, 1)
        before = pltpu.roll(v, 1, 0).reshape(grid.shape)
        after = pltpu.roll(v, v.shape[0] - 1, 0).reshape(grid.shape)
        taps = (
            jnp.where(column == 0, 0.0, before).reshape(v.shape),
            v,
            jnp.where(column == cols - 1, 0.0, after).reshape(v.shape),
        )
        inner = v.shape[0] - 2 * cols
        for c, tap in enumerate(taps):
            even[stage][c] = tap.astype(jnp.bfloat16)
            odd[stage][c] = tap[cols:cols + inner].astype(jnp.bfloat16)

    def spatial(stage):
        size = odd[stage].shape[1]
        lhs, rhs = [], []
        for c in (1, 0, 2):
            lhs += [even[stage][c, 0:size], odd[stage][c], even[stage][c, 2 * cols:2 * cols + size]]
            rhs += [ws[stage, (3 * r + c) * channels:(3 * r + c + 1) * channels] for r in range(3)]
        return jnp.dot(
            jnp.concatenate(lhs, -1), jnp.concatenate(rhs, 0), preferred_element_type=jnp.float32
        )

    def conv(v, stage, first):
        cache = caches[stage]
        if first:
            spread(v, stage)
            w_copies(stage)[0].wait()
            now = spatial(stage).astype(jnp.bfloat16)
            w_copies(stage)[1].wait()
            past = jnp.dot(
                jnp.concatenate([now, now], -1), wt[stage, :2 * channels],
                preferred_element_type=jnp.float32,
            )
            cache[0] = now
            cache[1] = now
        else:
            older, newer = cache[0], cache[1]
            past = jnp.dot(
                jnp.concatenate([older, newer], -1), wt[stage, :2 * channels],
                preferred_element_type=jnp.float32,
            )
            spread(v, stage)
            now = spatial(stage).astype(jnp.bfloat16)
            cache[0] = newer
            cache[1] = now
        return past + jnp.dot(now, wt[stage, 2 * channels:], preferred_element_type=jnp.float32)

    deep = depth_ref[0] > 1
    forward(0)

    def tick(f, first):
        @pl.when(has_left)
        def _():
            r_copy(f).wait_recv()

        @pl.when(has_right)
        def _():
            l_copy(f).wait_recv()

        x = jnp.concatenate([left[f], own[f], right[f]], 0).astype(jnp.float32)
        b = edge_rows(silu(conv(silu(x), 0, first)), 3 * cols, has_left, has_right)
        x1 = (x[2 * cols:-2 * cols] + conv(b, 1, first)).astype(jnp.bfloat16).astype(jnp.float32)
        x1 = edge_rows(x1, 2 * cols, has_left, has_right)

        @pl.when(f + 1 < frames)
        def _():
            forward(f + 1)

        b = edge_rows(silu(conv(silu(x1), 2, first)), cols, has_left, has_right)
        mid = x1[2 * cols:-2 * cols]
        x2 = mid + conv(b, 3, first)
        out_ref[f] = jnp.where(deep, x2, mid).astype(jnp.bfloat16)

        @pl.when(has_next)
        def _():
            z_copy(f).start()

    tick(0, True)

    def later(f, carry):
        tick(f, False)
        return carry

    lax.fori_loop(1, frames, later, 0)

    def drain(f, carry):
        @pl.when(has_next)
        def _():
            z_copy(f).wait_send()

        @pl.when(has_left)
        def _():
            l_copy(f).wait_send()

        @pl.when(has_right)
        def _():
            r_copy(f).wait_send()

        return carry

    lax.fori_loop(0, frames, drain, 0)


def per_device(segments, spaces, video, spatial_weight, temporal_weight, section_blocks):
    micro, frames, rows, cols, channels = video.shape
    steps = micro * frames
    cells = rows * cols
    spatial_set = spatial_weight.reshape(4, 9 * channels, channels)
    temporal_set = temporal_weight.reshape(4, 3 * channels, channels)
    bf16 = jnp.bfloat16
    sizes = [(3 * rows - 2 * i) * cols for i in range(5)]
    dma = pltpu.SemaphoreType.DMA
    out = pl.pallas_call(
        functools.partial(kernel, segments, spaces, rows, cols),
        out_shape=jax.ShapeDtypeStruct((steps, cells, channels), bf16),
        in_specs=[
            pl.BlockSpec(memory_space=pltpu.SMEM),
            pl.BlockSpec(memory_space=pltpu.VMEM),
            pl.BlockSpec(memory_space=pl.ANY),
            pl.BlockSpec(memory_space=pl.ANY),
        ],
        out_specs=pl.BlockSpec(memory_space=pltpu.VMEM),
        scratch_shapes=[
            pltpu.VMEM((steps, cells, channels), bf16),
            pltpu.VMEM((steps, cells, channels), bf16),
            pltpu.VMEM((steps, cells, channels), bf16),
            pltpu.VMEM(spatial_set.shape, bf16),
            pltpu.VMEM(temporal_set.shape, bf16),
            [pltpu.VMEM((3, sizes[i], channels), bf16) for i in range(4)],
            [pltpu.VMEM((3, sizes[i + 1], channels), bf16) for i in range(4)],
            [pltpu.VMEM((2, sizes[i + 1], channels), bf16) for i in range(4)],
            dma((8,)),
            dma((steps,)), dma((steps,)), dma((steps,)),
            dma((steps,)), dma((steps,)), dma((steps,)),
        ],
        compiler_params=pltpu.CompilerParams(
            collective_id=0, has_side_effects=True, vmem_limit_bytes=60 * 2**20
        ),
        name="sections",
    )(section_blocks, video.reshape(steps, cells, channels), spatial_set, temporal_set)
    return out.reshape(1, micro, frames, rows, cols, channels)


def solution(mesh):
    return jax.shard_map(
        functools.partial(per_device, mesh.shape["segment"], mesh.shape["space"]),
        mesh=mesh,
        in_specs=(
            P(None, None, "space", None, None),
            P("segment", None, None, None, None),
            P("segment", None, None, None, None),
            P("segment"),
        ),
        out_specs=P("segment", None, None, "space", None, None),
        check_vma=False,
    )
```

```python
import functools

import jax
import jax.numpy as jnp
from jax import lax
from jax.experimental import pallas as pl
from jax.experimental.pallas import tpu as pltpu
from jax.sharding import PartitionSpec as P

MESH = pl.DeviceIdType.MESH


def silu(v):
    half = 0.5 * v
    return half + half * jnp.tanh(half)


def edge_rows(v, width, low_ok, high_ok):
    low = jnp.where(low_ok, v[:width], 0.0)
    high = jnp.where(high_ok, v[-width:], 0.0)
    return jnp.concatenate([low, v[width:-width], high], 0)


def kernel(
    segments, spaces, rows, cols,
    depth_ref, video_ref, ws_hbm, wt_hbm, out_ref,
    own, left, right, ws, wt, caches,
    w_sem, z_send, z_recv, l_send, l_recv, r_send, r_recv,
):
    frames, cells, channels = video_ref.shape
    place = lax.axis_index("segment")
    spot = lax.axis_index("space")
    has_left = spot > 0
    has_right = spot < spaces - 1
    has_prev = place > 0
    has_next = place < segments - 1

    def w_copies(i):
        return (
            pltpu.make_async_copy(ws_hbm.at[i], ws.at[i], w_sem.at[2 * i]),
            pltpu.make_async_copy(wt_hbm.at[i], wt.at[i], w_sem.at[2 * i + 1]),
        )

    for i in range(4):
        for c in w_copies(i):
            c.start()

    to_next = {"segment": place + 1}
    to_prev = {"segment": place - 1}
    to_left = {"space": spot - 1}
    to_right = {"space": spot + 1}
    partners = ((has_prev, to_prev), (has_next, to_next), (has_left, to_left), (has_right, to_right))

    barrier = pltpu.get_barrier_semaphore()
    for there, target in partners:
        @pl.when(there)
        def _():
            pl.semaphore_signal(barrier, inc=1, device_id=target, device_id_type=MESH)

    @pl.when(place == 0)
    def _():
        own[...] = video_ref[...]

    @pl.when(spot == 0)
    def _():
        left[...] = jnp.zeros_like(left)

    @pl.when(spot == spaces - 1)
    def _():
        right[...] = jnp.zeros_like(right)

    peers = sum(there.astype(jnp.int32) for there, _target in partners)
    pl.semaphore_wait(barrier, peers)

    def z_copy(f):
        return pltpu.make_async_remote_copy(
            out_ref.at[f], own.at[f], z_send.at[f], z_recv.at[f],
            device_id=to_next, device_id_type=MESH,
        )

    def l_copy(f):
        return pltpu.make_async_remote_copy(
            own.at[f], right.at[f], l_send.at[f], l_recv.at[f],
            device_id=to_left, device_id_type=MESH,
        )

    def r_copy(f):
        return pltpu.make_async_remote_copy(
            own.at[f], left.at[f], r_send.at[f], r_recv.at[f],
            device_id=to_right, device_id_type=MESH,
        )

    def forward(f):
        @pl.when(has_prev)
        def _():
            z_copy(f).wait_recv()

        @pl.when(has_left)
        def _():
            l_copy(f).start()

        @pl.when(has_right)
        def _():
            r_copy(f).start()

    def spatial(v, stage):
        grid = (v.shape[0] // cols, cols, channels)
        size = v.shape[0] - 2 * cols
        column = lax.broadcasted_iota(jnp.int32, grid, 1)
        before = pltpu.roll(v, 1, 0).reshape(grid)
        after = pltpu.roll(v, v.shape[0] - 1, 0).reshape(grid)
        taps = (
            jnp.where(column == 0, 0.0, before).reshape(v.shape),
            v,
            jnp.where(column == cols - 1, 0.0, after).reshape(v.shape),
        )
        lhs, rhs = [], []
        for c in (1, 0, 2):
            even = taps[c].astype(jnp.bfloat16)
            odd = taps[c][cols:cols + size].astype(jnp.bfloat16)
            lhs += [even[:size], odd, even[2 * cols:]]
            rhs += [ws[stage, (3 * r + c) * channels:(3 * r + c + 1) * channels] for r in range(3)]
        return jnp.dot(
            jnp.concatenate(lhs, -1), jnp.concatenate(rhs, 0), preferred_element_type=jnp.float32
        )

    def conv(v, stage, first):
        cache = caches[stage]
        wide = jnp.float32
        if first:
            w_copies(stage)[0].wait()
            now = spatial(v, stage).astype(jnp.bfloat16)
            w_copies(stage)[1].wait()
            past = jnp.dot(
                jnp.concatenate([now, now], -1), wt[stage, :2 * channels], preferred_element_type=wide
            )
            cache[0] = now.astype(wide)
        else:
            older, newer = cache[0], cache[1]
            past = jnp.dot(
                jnp.concatenate([older, newer], -1).astype(jnp.bfloat16), wt[stage, :2 * channels],
                preferred_element_type=wide,
            )
            now = spatial(v, stage).astype(jnp.bfloat16)
            cache[0] = newer
        cache[1] = now.astype(wide)
        return past + jnp.dot(now, wt[stage, 2 * channels:], preferred_element_type=wide)

    deep = depth_ref[0] > 1
    forward(0)

    def tick(f, first):
        @pl.when(has_left)
        def _():
            r_copy(f).wait_recv()

        @pl.when(has_right)
        def _():
            l_copy(f).wait_recv()

        x = jnp.concatenate([left[f], own[f], right[f]], 0).astype(jnp.float32)
        b = edge_rows(silu(conv(silu(x), 0, first)), 3 * cols, has_left, has_right)
        x1 = (x[2 * cols:-2 * cols] + conv(b, 1, first)).astype(jnp.bfloat16).astype(jnp.float32)
        x1 = edge_rows(x1, 2 * cols, has_left, has_right)

        @pl.when(f + 1 < frames)
        def _():
            forward(f + 1)

        b = edge_rows(silu(conv(silu(x1), 2, first)), cols, has_left, has_right)
        mid = x1[2 * cols:-2 * cols]
        x2 = mid + conv(b, 3, first)
        out_ref[f] = jnp.where(deep, x2, mid).astype(jnp.bfloat16)

        @pl.when(has_next)
        def _():
            z_copy(f).start()

    tick(0, True)

    def later(f, carry):
        tick(f, False)
        return carry

    lax.fori_loop(1, frames, later, 0)

    def drain(f, carry):
        @pl.when(has_next)
        def _():
            z_copy(f).wait_send()

        @pl.when(has_left)
        def _():
            l_copy(f).wait_send()

        @pl.when(has_right)
        def _():
            r_copy(f).wait_send()

        return carry

    lax.fori_loop(0, frames, drain, 0)


def per_device(segments, spaces, video, spatial_weight, temporal_weight, section_blocks):
    micro, frames, rows, cols, channels = video.shape
    steps = micro * frames
    cells = rows * cols
    spatial_set = spatial_weight.reshape(4, 9 * channels, channels)
    temporal_set = temporal_weight.reshape(4, 3 * channels, channels)
    bf16 = jnp.bfloat16
    sizes = [(3 * rows - 2 * i) * cols for i in range(5)]
    dma = pltpu.SemaphoreType.DMA
    out = pl.pallas_call(
        functools.partial(kernel, segments, spaces, rows, cols),
        out_shape=jax.ShapeDtypeStruct((steps, cells, channels), bf16),
        in_specs=[
            pl.BlockSpec(memory_space=pltpu.SMEM),
            pl.BlockSpec(memory_space=pltpu.VMEM),
            pl.BlockSpec(memory_space=pl.ANY),
            pl.BlockSpec(memory_space=pl.ANY),
        ],
        out_specs=pl.BlockSpec(memory_space=pltpu.VMEM),
        scratch_shapes=[
            pltpu.VMEM((steps, cells, channels), bf16),
            pltpu.VMEM((steps, cells, channels), bf16),
            pltpu.VMEM((steps, cells, channels), bf16),
            pltpu.VMEM(spatial_set.shape, bf16),
            pltpu.VMEM(temporal_set.shape, bf16),
            [pltpu.VMEM((2, sizes[i + 1], channels), jnp.float32) for i in range(4)],
            dma((8,)),
            dma((steps,)), dma((steps,)), dma((steps,)),
            dma((steps,)), dma((steps,)), dma((steps,)),
        ],
        compiler_params=pltpu.CompilerParams(
            collective_id=0, has_side_effects=True, vmem_limit_bytes=60 * 2**20
        ),
        name="sections",
    )(section_blocks, video.reshape(steps, cells, channels), spatial_set, temporal_set)
    return out.reshape(1, micro, frames, rows, cols, channels)


def solution(mesh):
    return jax.shard_map(
        functools.partial(per_device, mesh.shape["segment"], mesh.shape["space"]),
        mesh=mesh,
        in_specs=(
            P(None, None, "space", None, None),
            P("segment", None, None, None, None),
            P("segment", None, None, None, None),
            P("segment"),
        ),
        out_specs=P("segment", None, None, "space", None, None),
        check_vma=False,
    )
```

```python
import functools

import jax
import jax.numpy as jnp
from jax import lax
from jax.experimental import pallas as pl
from jax.experimental.pallas import tpu as pltpu
from jax.sharding import PartitionSpec as P

MESH = pl.DeviceIdType.MESH
GROUP = 2


def silu(v):
    half = 0.5 * v
    return half + half * jnp.tanh(half)


def edge_rows(v, width, low_ok, high_ok):
    low = jnp.where(low_ok, v[:width], 0.0)
    high = jnp.where(high_ok, v[-width:], 0.0)
    return jnp.concatenate([low, v[width:-width], high], 0)


def kernel(
    segments, spaces, rows, cols,
    depth_ref, video_ref, ws_hbm, wt_hbm, out_ref,
    own, left, right, ws, wt, caches,
    w_sem, z_send, z_recv, l_send, l_recv, r_send, r_recv,
):
    ticks = video_ref.shape[0]
    cells = rows * cols
    group = video_ref.shape[1] // cells
    channels = video_ref.shape[2]
    place = lax.axis_index("segment")
    spot = lax.axis_index("space")
    has_left = spot > 0
    has_right = spot < spaces - 1
    has_prev = place > 0
    has_next = place < segments - 1

    def w_copies(i):
        return (
            pltpu.make_async_copy(ws_hbm.at[i], ws.at[i], w_sem.at[2 * i]),
            pltpu.make_async_copy(wt_hbm.at[i], wt.at[i], w_sem.at[2 * i + 1]),
        )

    for i in range(4):
        for c in w_copies(i):
            c.start()

    to_next = {"segment": place + 1}
    to_prev = {"segment": place - 1}
    to_left = {"space": spot - 1}
    to_right = {"space": spot + 1}
    partners = ((has_prev, to_prev), (has_next, to_next), (has_left, to_left), (has_right, to_right))

    barrier = pltpu.get_barrier_semaphore()
    for there, target in partners:
        @pl.when(there)
        def _():
            pl.semaphore_signal(barrier, inc=1, device_id=target, device_id_type=MESH)

    @pl.when(place == 0)
    def _():
        own[...] = video_ref[...]

    @pl.when(spot == 0)
    def _():
        left[...] = jnp.zeros_like(left)

    @pl.when(spot == spaces - 1)
    def _():
        right[...] = jnp.zeros_like(right)

    peers = sum(there.astype(jnp.int32) for there, _target in partners)
    pl.semaphore_wait(barrier, peers)

    def z_copy(f):
        return pltpu.make_async_remote_copy(
            out_ref.at[f], own.at[f], z_send.at[f], z_recv.at[f],
            device_id=to_next, device_id_type=MESH,
        )

    def l_copy(f):
        return pltpu.make_async_remote_copy(
            own.at[f], right.at[f], l_send.at[f], l_recv.at[f],
            device_id=to_left, device_id_type=MESH,
        )

    def r_copy(f):
        return pltpu.make_async_remote_copy(
            own.at[f], left.at[f], r_send.at[f], r_recv.at[f],
            device_id=to_right, device_id_type=MESH,
        )

    def start_halo(f):
        @pl.when(has_left)
        def _():
            l_copy(f).start()

        @pl.when(has_right)
        def _():
            r_copy(f).start()

    def forward(f):
        @pl.when(has_prev)
        def _():
            z_copy(f).wait_recv()
            start_halo(f)

    def taps(v):
        grid = (v.shape[0] // cols, cols, channels)
        size = v.shape[0] - 2 * cols
        column = lax.broadcasted_iota(jnp.int32, grid, 1)
        before = pltpu.roll(v, 1, 0).reshape(grid)
        after = pltpu.roll(v, v.shape[0] - 1, 0).reshape(grid)
        shifted = (
            jnp.where(column == 0, 0.0, before).reshape(v.shape),
            v,
            jnp.where(column == cols - 1, 0.0, after).reshape(v.shape),
        )
        pieces = []
        for c in (1, 0, 2):
            even = shifted[c].astype(jnp.bfloat16)
            odd = shifted[c][cols:cols + size].astype(jnp.bfloat16)
            pieces += [even[:size], odd, even[2 * cols:]]
        return jnp.concatenate(pieces, -1)

    def conv(vs, stage, first):
        cache = caches[stage]
        wide = jnp.float32
        size = vs[0].shape[0] - 2 * cols
        if first:
            w_copies(stage)[0].wait()
        lhs = jnp.concatenate([taps(v) for v in vs], 0)
        rhs = jnp.concatenate(
            [ws[stage, (3 * r + c) * channels:(3 * r + c + 1) * channels] for c in (1, 0, 2) for r in range(3)], 0
        )
        now = jnp.dot(lhs, rhs, preferred_element_type=wide).astype(jnp.bfloat16)
        nows = [now[g * size:(g + 1) * size] for g in range(len(vs))]
        if first:
            w_copies(stage)[1].wait()
            line = [nows[0], nows[0]] + nows
        else:
            line = [cache[0].astype(jnp.bfloat16), cache[1].astype(jnp.bfloat16)] + nows
        cache[0] = line[-2].astype(wide)
        cache[1] = line[-1].astype(wide)
        lhs = jnp.concatenate(
            [jnp.concatenate(line[g:g + 3], -1) for g in range(len(vs))], 0
        )
        mixed = jnp.dot(lhs, wt[stage], preferred_element_type=wide)
        return [mixed[g * size:(g + 1) * size] for g in range(len(vs))]

    deep = depth_ref[0] > 1

    @pl.when(place == 0)
    def _():
        def send(f, carry):
            start_halo(f)
            return carry

        lax.fori_loop(0, ticks, send, 0)

    forward(0)

    def tick(f, first):
        @pl.when(has_left)
        def _():
            r_copy(f).wait_recv()

        @pl.when(has_right)
        def _():
            l_copy(f).wait_recv()

        xs = []
        for g in range(group):
            span = slice(g * cells, (g + 1) * cells)
            xs.append(jnp.concatenate([left[f, span], own[f, span], right[f, span]], 0).astype(jnp.float32))
        bs = [edge_rows(silu(q), 3 * cols, has_left, has_right) for q in conv([silu(x) for x in xs], 0, first)]
        qs = conv(bs, 1, first)
        x1s = [(x[2 * cols:-2 * cols] + q).astype(jnp.bfloat16).astype(jnp.float32) for x, q in zip(xs, qs)]
        x1s = [edge_rows(x1, 2 * cols, has_left, has_right) for x1 in x1s]

        @pl.when(f + 1 < ticks)
        def _():
            forward(f + 1)

        bs = [edge_rows(silu(q), cols, has_left, has_right) for q in conv([silu(x) for x in x1s], 2, first)]
        qs = conv(bs, 3, first)
        for g in range(group):
            mid = x1s[g][2 * cols:-2 * cols]
            out_ref[f, g * cells:(g + 1) * cells] = jnp.where(deep, mid + qs[g], mid).astype(jnp.bfloat16)

        @pl.when(has_next)
        def _():
            z_copy(f).start()

    tick(0, True)

    def later(f, carry):
        tick(f, False)
        return carry

    lax.fori_loop(1, ticks, later, 0)

    def drain(f, carry):
        @pl.when(has_next)
        def _():
            z_copy(f).wait_send()

        @pl.when(has_left)
        def _():
            l_copy(f).wait_send()

        @pl.when(has_right)
        def _():
            r_copy(f).wait_send()

        return carry

    lax.fori_loop(0, ticks, drain, 0)


def per_device(segments, spaces, video, spatial_weight, temporal_weight, section_blocks):
    micro, frames, rows, cols, channels = video.shape
    steps = micro * frames // GROUP
    cells = GROUP * rows * cols
    spatial_set = spatial_weight.reshape(4, 9 * channels, channels)
    temporal_set = temporal_weight.reshape(4, 3 * channels, channels)
    bf16 = jnp.bfloat16
    sizes = [(3 * rows - 2 * i) * cols for i in range(5)]
    dma = pltpu.SemaphoreType.DMA
    out = pl.pallas_call(
        functools.partial(kernel, segments, spaces, rows, cols),
        out_shape=jax.ShapeDtypeStruct((steps, cells, channels), bf16),
        in_specs=[
            pl.BlockSpec(memory_space=pltpu.SMEM),
            pl.BlockSpec(memory_space=pltpu.VMEM),
            pl.BlockSpec(memory_space=pl.ANY),
            pl.BlockSpec(memory_space=pl.ANY),
        ],
        out_specs=pl.BlockSpec(memory_space=pltpu.VMEM),
        scratch_shapes=[
            pltpu.VMEM((steps, cells, channels), bf16),
            pltpu.VMEM((steps, cells, channels), bf16),
            pltpu.VMEM((steps, cells, channels), bf16),
            pltpu.VMEM(spatial_set.shape, bf16),
            pltpu.VMEM(temporal_set.shape, bf16),
            [pltpu.VMEM((2, sizes[i + 1], channels), jnp.float32) for i in range(4)],
            dma((8,)),
            dma((steps,)), dma((steps,)), dma((steps,)),
            dma((steps,)), dma((steps,)), dma((steps,)),
        ],
        compiler_params=pltpu.CompilerParams(
            collective_id=0, has_side_effects=True, vmem_limit_bytes=60 * 2**20
        ),
        name="sections",
    )(section_blocks, video.reshape(steps, cells, channels), spatial_set, temporal_set)
    return out.reshape(1, micro, frames, rows, cols, channels)


def solution(mesh):
    return jax.shard_map(
        functools.partial(per_device, mesh.shape["segment"], mesh.shape["space"]),
        mesh=mesh,
        in_specs=(
            P(None, None, "space", None, None),
            P("segment", None, None, None, None),
            P("segment", None, None, None, None),
            P("segment"),
        ),
        out_specs=P("segment", None, None, "space", None, None),
        check_vma=False,
    )
```

```python
import functools

import jax
import jax.numpy as jnp
from jax import lax
from jax.experimental import pallas as pl
from jax.experimental.pallas import tpu as pltpu
from jax.sharding import PartitionSpec as P

MESH = pl.DeviceIdType.MESH
GROUP = 1


def silu(v):
    half = 0.5 * v
    return half + half * jnp.tanh(half)


def edge_rows(v, width, low_ok, high_ok):
    low = jnp.where(low_ok, v[:width], 0.0)
    high = jnp.where(high_ok, v[-width:], 0.0)
    return jnp.concatenate([low, v[width:-width], high], 0)


def kernel(
    segments, spaces, rows, cols,
    depth_ref, video_ref, ws_hbm, wt_hbm, out_ref,
    own, left, right, ws_raw, wt_raw, ws, wt, caches,
    w_sem, z_send, z_recv, l_send, l_recv, r_send, r_recv,
):
    ticks = video_ref.shape[0]
    cells = rows * cols
    group = video_ref.shape[1] // cells
    channels = video_ref.shape[2]
    place = lax.axis_index("segment")
    spot = lax.axis_index("space")
    has_left = spot > 0
    has_right = spot < spaces - 1
    has_prev = place > 0
    has_next = place < segments - 1

    def w_copies(i):
        return (
            pltpu.make_async_copy(ws_hbm.at[i], ws_raw.at[i], w_sem.at[2 * i]),
            pltpu.make_async_copy(wt_hbm.at[i], wt_raw.at[i], w_sem.at[2 * i + 1]),
        )

    for i in range(4):
        for c in w_copies(i):
            c.start()

    to_next = {"segment": place + 1}
    to_prev = {"segment": place - 1}
    to_left = {"space": spot - 1}
    to_right = {"space": spot + 1}
    partners = ((has_prev, to_prev), (has_next, to_next), (has_left, to_left), (has_right, to_right))

    barrier = pltpu.get_barrier_semaphore()
    for there, target in partners:
        @pl.when(there)
        def _():
            pl.semaphore_signal(barrier, inc=1, device_id=target, device_id_type=MESH)

    @pl.when(place == 0)
    def _():
        own[...] = video_ref[...]

    @pl.when(spot == 0)
    def _():
        left[...] = jnp.zeros_like(left)

    @pl.when(spot == spaces - 1)
    def _():
        right[...] = jnp.zeros_like(right)

    peers = sum(there.astype(jnp.int32) for there, _target in partners)
    pl.semaphore_wait(barrier, peers)

    def z_copy(f):
        return pltpu.make_async_remote_copy(
            out_ref.at[f], own.at[f], z_send.at[f], z_recv.at[f],
            device_id=to_next, device_id_type=MESH,
        )

    def l_copy(f):
        return pltpu.make_async_remote_copy(
            own.at[f], right.at[f], l_send.at[f], l_recv.at[f],
            device_id=to_left, device_id_type=MESH,
        )

    def r_copy(f):
        return pltpu.make_async_remote_copy(
            own.at[f], left.at[f], r_send.at[f], r_recv.at[f],
            device_id=to_right, device_id_type=MESH,
        )

    def start_halo(f):
        @pl.when(has_left)
        def _():
            l_copy(f).start()

        @pl.when(has_right)
        def _():
            r_copy(f).start()

    def forward(f):
        @pl.when(has_prev)
        def _():
            z_copy(f).wait_recv()
            start_halo(f)

    def taps(v):
        grid = (v.shape[0] // cols, cols, channels)
        size = v.shape[0] - 2 * cols
        column = lax.broadcasted_iota(jnp.int32, grid, 1)
        before = pltpu.roll(v, 1, 0).reshape(grid)
        after = pltpu.roll(v, v.shape[0] - 1, 0).reshape(grid)
        shifted = (
            jnp.where(column == 0, 0.0, before).reshape(v.shape),
            v,
            jnp.where(column == cols - 1, 0.0, after).reshape(v.shape),
        )
        pieces = []
        for c in (1, 0, 2):
            even = shifted[c].astype(jnp.bfloat16)
            odd = shifted[c][cols:cols + size].astype(jnp.bfloat16)
            pieces += [even[:size], odd, even[2 * cols:]]
        return jnp.concatenate(pieces, -1)

    def conv(vs, stage, first):
        cache = caches[stage]
        wide = jnp.float32
        size = vs[0].shape[0] - 2 * cols
        if first:
            w_copies(stage)[0].wait()
            ws[stage] = ws_raw[stage].astype(wide)
        lhs = jnp.concatenate([taps(v) for v in vs], 0)
        rhs = jnp.concatenate(
            [ws[stage, (3 * r + c) * channels:(3 * r + c + 1) * channels] for c in (1, 0, 2) for r in range(3)], 0
        ).astype(jnp.bfloat16)
        now = jnp.dot(lhs, rhs, preferred_element_type=wide).astype(jnp.bfloat16)
        nows = [now[g * size:(g + 1) * size] for g in range(len(vs))]
        if first:
            w_copies(stage)[1].wait()
            wt[stage] = wt_raw[stage].astype(wide)
            line = [nows[0], nows[0]] + nows
        else:
            line = [cache[0].astype(jnp.bfloat16), cache[1].astype(jnp.bfloat16)] + nows
        cache[0] = line[-2].astype(wide)
        cache[1] = line[-1].astype(wide)
        lhs = jnp.concatenate(
            [jnp.concatenate(line[g:g + 3], -1) for g in range(len(vs))], 0
        )
        mixed = jnp.dot(lhs, wt[stage].astype(jnp.bfloat16), preferred_element_type=wide)
        return [mixed[g * size:(g + 1) * size] for g in range(len(vs))]

    deep = depth_ref[0] > 1

    @pl.when(place == 0)
    def _():
        def send(f, carry):
            start_halo(f)
            return carry

        lax.fori_loop(0, ticks, send, 0)

    forward(0)

    def tick(f, first):
        @pl.when(has_left)
        def _():
            r_copy(f).wait_recv()

        @pl.when(has_right)
        def _():
            l_copy(f).wait_recv()

        xs = []
        for g in range(group):
            span = slice(g * cells, (g + 1) * cells)
            xs.append(jnp.concatenate([left[f, span], own[f, span], right[f, span]], 0).astype(jnp.float32))
        bs = [edge_rows(silu(q), 3 * cols, has_left, has_right) for q in conv([silu(x) for x in xs], 0, first)]
        @pl.when(f + 1 < ticks)
        def _():
            forward(f + 1)

        qs = conv(bs, 1, first)
        x1s = [(x[2 * cols:-2 * cols] + q).astype(jnp.bfloat16).astype(jnp.float32) for x, q in zip(xs, qs)]
        x1s = [edge_rows(x1, 2 * cols, has_left, has_right) for x1 in x1s]

        bs = [edge_rows(silu(q), cols, has_left, has_right) for q in conv([silu(x) for x in x1s], 2, first)]
        qs = conv(bs, 3, first)
        for g in range(group):
            mid = x1s[g][2 * cols:-2 * cols]
            out_ref[f, g * cells:(g + 1) * cells] = jnp.where(deep, mid + qs[g], mid).astype(jnp.bfloat16)

        @pl.when(has_next)
        def _():
            z_copy(f).start()

    tick(0, True)

    def later(f, carry):
        tick(f, False)
        return carry

    lax.fori_loop(1, ticks, later, 0)

    def drain(f, carry):
        @pl.when(has_next)
        def _():
            z_copy(f).wait_send()

        @pl.when(has_left)
        def _():
            l_copy(f).wait_send()

        @pl.when(has_right)
        def _():
            r_copy(f).wait_send()

        return carry

    lax.fori_loop(0, ticks, drain, 0)


def per_device(segments, spaces, video, spatial_weight, temporal_weight, section_blocks):
    micro, frames, rows, cols, channels = video.shape
    steps = micro * frames // GROUP
    cells = GROUP * rows * cols
    spatial_set = spatial_weight.reshape(4, 9 * channels, channels)
    temporal_set = temporal_weight.reshape(4, 3 * channels, channels)
    bf16 = jnp.bfloat16
    sizes = [(3 * rows - 2 * i) * cols for i in range(5)]
    dma = pltpu.SemaphoreType.DMA
    out = pl.pallas_call(
        functools.partial(kernel, segments, spaces, rows, cols),
        out_shape=jax.ShapeDtypeStruct((steps, cells, channels), bf16),
        in_specs=[
            pl.BlockSpec(memory_space=pltpu.SMEM),
            pl.BlockSpec(memory_space=pltpu.VMEM),
            pl.BlockSpec(memory_space=pl.ANY),
            pl.BlockSpec(memory_space=pl.ANY),
        ],
        out_specs=pl.BlockSpec(memory_space=pltpu.VMEM),
        scratch_shapes=[
            pltpu.VMEM((steps, cells, channels), bf16),
            pltpu.VMEM((steps, cells, channels), bf16),
            pltpu.VMEM((steps, cells, channels), bf16),
            pltpu.VMEM(spatial_set.shape, bf16),
            pltpu.VMEM(temporal_set.shape, bf16),
            pltpu.VMEM(spatial_set.shape, jnp.float32),
            pltpu.VMEM(temporal_set.shape, jnp.float32),
            [pltpu.VMEM((2, sizes[i + 1], channels), jnp.float32) for i in range(4)],
            dma((8,)),
            dma((steps,)), dma((steps,)), dma((steps,)),
            dma((steps,)), dma((steps,)), dma((steps,)),
        ],
        compiler_params=pltpu.CompilerParams(
            collective_id=0, has_side_effects=True, vmem_limit_bytes=60 * 2**20
        ),
        name="sections",
    )(section_blocks, video.reshape(steps, cells, channels), spatial_set, temporal_set)
    return out.reshape(1, micro, frames, rows, cols, channels)


def solution(mesh):
    return jax.shard_map(
        functools.partial(per_device, mesh.shape["segment"], mesh.shape["space"]),
        mesh=mesh,
        in_specs=(
            P(None, None, "space", None, None),
            P("segment", None, None, None, None),
            P("segment", None, None, None, None),
            P("segment"),
        ),
        out_specs=P("segment", None, None, "space", None, None),
        check_vma=False,
    )
```

```python
import functools

import jax
import jax.numpy as jnp
from jax import lax
from jax.experimental import pallas as pl
from jax.experimental.pallas import tpu as pltpu
from jax.sharding import PartitionSpec as P

MESH = pl.DeviceIdType.MESH
GROUP = 1


def silu(v):
    half = 0.5 * v
    return half + half * jnp.tanh(half)


def edge_rows(v, width, low_ok, high_ok):
    low = jnp.where(low_ok, v[:width], 0.0)
    high = jnp.where(high_ok, v[-width:], 0.0)
    return jnp.concatenate([low, v[width:-width], high], 0)


def kernel(
    segments, spaces, rows, cols,
    depth_ref, video_ref, ws_hbm, wt_hbm, out_ref,
    own, left, right, ws, wt, caches,
    w_sem, z_send, z_recv, l_send, l_recv, r_send, r_recv,
):
    ticks = video_ref.shape[0]
    cells = rows * cols
    group = video_ref.shape[1] // cells
    channels = video_ref.shape[2]
    halves = channels // 128
    place = lax.axis_index("segment")
    spot = lax.axis_index("space")
    has_left = spot > 0
    has_right = spot < spaces - 1
    has_prev = place > 0
    has_next = place < segments - 1

    def w_copies(i, which):
        source, target = ((ws_hbm, ws), (wt_hbm, wt))[which]
        return [
            pltpu.make_async_copy(
                source.at[i, :, pl.ds(128 * h, 128)], target.at[h, i], w_sem.at[(2 * i + which) * halves + h]
            )
            for h in range(halves)
        ]

    for i in range(4):
        for c in w_copies(i, 0) + w_copies(i, 1):
            c.start()

    to_next = {"segment": place + 1}
    to_prev = {"segment": place - 1}
    to_left = {"space": spot - 1}
    to_right = {"space": spot + 1}
    partners = ((has_prev, to_prev), (has_next, to_next), (has_left, to_left), (has_right, to_right))

    barrier = pltpu.get_barrier_semaphore()
    for there, target in partners:
        @pl.when(there)
        def _():
            pl.semaphore_signal(barrier, inc=1, device_id=target, device_id_type=MESH)

    @pl.when(place == 0)
    def _():
        own[...] = video_ref[...]

    @pl.when(spot == 0)
    def _():
        left[...] = jnp.zeros_like(left)

    @pl.when(spot == spaces - 1)
    def _():
        right[...] = jnp.zeros_like(right)

    peers = sum(there.astype(jnp.int32) for there, _target in partners)
    pl.semaphore_wait(barrier, peers)

    def z_copy(f):
        return pltpu.make_async_remote_copy(
            out_ref.at[f], own.at[f], z_send.at[f], z_recv.at[f],
            device_id=to_next, device_id_type=MESH,
        )

    def l_copy(f):
        return pltpu.make_async_remote_copy(
            own.at[f], right.at[f], l_send.at[f], l_recv.at[f],
            device_id=to_left, device_id_type=MESH,
        )

    def r_copy(f):
        return pltpu.make_async_remote_copy(
            own.at[f], left.at[f], r_send.at[f], r_recv.at[f],
            device_id=to_right, device_id_type=MESH,
        )

    def start_halo(f):
        @pl.when(has_left)
        def _():
            l_copy(f).start()

        @pl.when(has_right)
        def _():
            r_copy(f).start()

    def forward(f):
        @pl.when(has_prev)
        def _():
            z_copy(f).wait_recv()

        start_halo(f)

    def taps(v):
        grid = (v.shape[0] // cols, cols, channels)
        size = v.shape[0] - 2 * cols
        column = lax.broadcasted_iota(jnp.int32, grid, 1)
        before = pltpu.roll(v, 1, 0).reshape(grid)
        after = pltpu.roll(v, v.shape[0] - 1, 0).reshape(grid)
        shifted = (
            jnp.where(column == 0, 0.0, before).reshape(v.shape),
            v,
            jnp.where(column == cols - 1, 0.0, after).reshape(v.shape),
        )
        pieces = []
        for c in (1, 0, 2):
            even = shifted[c].astype(jnp.bfloat16)
            odd = shifted[c][cols:cols + size].astype(jnp.bfloat16)
            pieces += [even[:size], odd, even[2 * cols:]]
        return jnp.concatenate(pieces, -1)

    def conv(vs, stage, first):
        cache = caches[stage]
        wide = jnp.float32
        size = vs[0].shape[0] - 2 * cols
        if first:
            for c in w_copies(stage, 0):
                c.wait()
        lhs = jnp.concatenate([taps(v) for v in vs], 0)
        kernels = jnp.concatenate([ws[h, stage] for h in range(halves)], -1)
        rhs = jnp.concatenate(
            [kernels[(3 * r + c) * channels:(3 * r + c + 1) * channels] for c in (1, 0, 2) for r in range(3)], 0
        )
        now = jnp.dot(lhs, rhs, preferred_element_type=wide).astype(jnp.bfloat16)
        nows = [now[g * size:(g + 1) * size] for g in range(len(vs))]
        if first:
            for c in w_copies(stage, 1):
                c.wait()
            line = [nows[0], nows[0]] + nows
        else:
            line = [cache[0].astype(jnp.bfloat16), cache[1].astype(jnp.bfloat16)] + nows
        cache[0] = line[-2].astype(wide)
        cache[1] = line[-1].astype(wide)
        lhs = jnp.concatenate(
            [jnp.concatenate(line[g:g + 3], -1) for g in range(len(vs))], 0
        )
        kernels = jnp.concatenate([wt[h, stage] for h in range(halves)], -1)
        mixed = jnp.dot(lhs, kernels, preferred_element_type=wide)
        return [mixed[g * size:(g + 1) * size] for g in range(len(vs))]

    deep = depth_ref[0] > 1

    forward(0)

    def tick(f, first):
        @pl.when(has_left)
        def _():
            r_copy(f).wait_recv()

        @pl.when(has_right)
        def _():
            l_copy(f).wait_recv()

        xs = []
        for g in range(group):
            span = slice(g * cells, (g + 1) * cells)
            xs.append(jnp.concatenate([left[f, span], own[f, span], right[f, span]], 0).astype(jnp.float32))
        bs = [edge_rows(silu(q), 3 * cols, has_left, has_right) for q in conv([silu(x) for x in xs], 0, first)]
        @pl.when(f + 1 < ticks)
        def _():
            forward(f + 1)

        qs = conv(bs, 1, first)
        x1s = [(x[2 * cols:-2 * cols] + q).astype(jnp.bfloat16).astype(jnp.float32) for x, q in zip(xs, qs)]
        x1s = [edge_rows(x1, 2 * cols, has_left, has_right) for x1 in x1s]

        bs = [edge_rows(silu(q), cols, has_left, has_right) for q in conv([silu(x) for x in x1s], 2, first)]
        qs = conv(bs, 3, first)
        for g in range(group):
            mid = x1s[g][2 * cols:-2 * cols]
            out_ref[f, g * cells:(g + 1) * cells] = jnp.where(deep, mid + qs[g], mid).astype(jnp.bfloat16)

        @pl.when(has_next)
        def _():
            z_copy(f).start()

    tick(0, True)

    def later(f, carry):
        tick(f, False)
        return carry

    lax.fori_loop(1, ticks, later, 0)

    def drain(f, carry):
        @pl.when(has_next)
        def _():
            z_copy(f).wait_send()

        @pl.when(has_left)
        def _():
            l_copy(f).wait_send()

        @pl.when(has_right)
        def _():
            r_copy(f).wait_send()

        return carry

    lax.fori_loop(0, ticks, drain, 0)


def per_device(segments, spaces, video, spatial_weight, temporal_weight, section_blocks):
    micro, frames, rows, cols, channels = video.shape
    steps = micro * frames // GROUP
    cells = GROUP * rows * cols
    spatial_set = spatial_weight.reshape(4, 9 * channels, channels)
    temporal_set = temporal_weight.reshape(4, 3 * channels, channels)
    bf16 = jnp.bfloat16
    sizes = [(3 * rows - 2 * i) * cols for i in range(5)]
    dma = pltpu.SemaphoreType.DMA
    out = pl.pallas_call(
        functools.partial(kernel, segments, spaces, rows, cols),
        out_shape=jax.ShapeDtypeStruct((steps, cells, channels), bf16),
        in_specs=[
            pl.BlockSpec(memory_space=pltpu.SMEM),
            pl.BlockSpec(memory_space=pltpu.VMEM),
            pl.BlockSpec(memory_space=pl.ANY),
            pl.BlockSpec(memory_space=pl.ANY),
        ],
        out_specs=pl.BlockSpec(memory_space=pltpu.VMEM),
        scratch_shapes=[
            pltpu.VMEM((steps, cells, channels), bf16),
            pltpu.VMEM((steps, cells, channels), bf16),
            pltpu.VMEM((steps, cells, channels), bf16),
            pltpu.VMEM((channels // 128, 4, 9 * channels, 128), bf16),
            pltpu.VMEM((channels // 128, 4, 3 * channels, 128), bf16),
            [pltpu.VMEM((2, sizes[i + 1], channels), jnp.float32) for i in range(4)],
            dma((8 * channels // 128,)),
            dma((steps,)), dma((steps,)), dma((steps,)),
            dma((steps,)), dma((steps,)), dma((steps,)),
        ],
        compiler_params=pltpu.CompilerParams(
            collective_id=0, has_side_effects=True, vmem_limit_bytes=60 * 2**20
        ),
        name="sections",
    )(section_blocks, video.reshape(steps, cells, channels), spatial_set, temporal_set)
    return out.reshape(1, micro, frames, rows, cols, channels)


def solution(mesh):
    return jax.shard_map(
        functools.partial(per_device, mesh.shape["segment"], mesh.shape["space"]),
        mesh=mesh,
        in_specs=(
            P(None, None, "space", None, None),
            P("segment", None, None, None, None),
            P("segment", None, None, None, None),
            P("segment"),
        ),
        out_specs=P("segment", None, None, "space", None, None),
        check_vma=False,
    )
```

```python
import functools

import jax
import jax.numpy as jnp
from jax import lax
from jax.experimental import pallas as pl
from jax.experimental.pallas import tpu as pltpu
from jax.sharding import PartitionSpec as P

MESH = pl.DeviceIdType.MESH
GROUP = 1


def silu(v):
    half = 0.5 * v
    return half + half * jnp.tanh(half)


def edge_rows(v, width, low_ok, high_ok):
    low = jnp.where(low_ok, v[:width], 0.0)
    high = jnp.where(high_ok, v[-width:], 0.0)
    return jnp.concatenate([low, v[width:-width], high], 0)


def kernel(
    segments, spaces, rows, cols,
    depth_ref, video_ref, ws_hbm, wt_hbm, out_ref,
    own, left, right, ws, wt, caches,
    w_sem, z_send, z_recv, l_send, l_recv, r_send, r_recv,
):
    ticks = video_ref.shape[0]
    cells = rows * cols
    group = video_ref.shape[1] // cells
    channels = video_ref.shape[2]
    halves = channels // 128
    place = lax.axis_index("segment")
    spot = lax.axis_index("space")
    has_left = spot > 0
    has_right = spot < spaces - 1
    has_prev = place > 0
    has_next = place < segments - 1

    def w_copies(i, which):
        source, target = ((ws_hbm, ws), (wt_hbm, wt))[which]
        return [
            pltpu.make_async_copy(
                source.at[i, :, pl.ds(128 * h, 128)], target.at[h, i], w_sem.at[(2 * i + which) * halves + h]
            )
            for h in range(halves)
        ]

    for i in range(4):
        for c in w_copies(i, 0) + w_copies(i, 1):
            c.start()

    to_next = {"segment": place + 1}
    to_prev = {"segment": place - 1}
    to_left = {"space": spot - 1}
    to_right = {"space": spot + 1}
    partners = ((has_prev, to_prev), (has_next, to_next), (has_left, to_left), (has_right, to_right))

    barrier = pltpu.get_barrier_semaphore()
    for there, target in partners:
        @pl.when(there)
        def _():
            pl.semaphore_signal(barrier, inc=1, device_id=target, device_id_type=MESH)

    @pl.when(place == 0)
    def _():
        own[...] = video_ref[...]

    @pl.when(spot == 0)
    def _():
        left[...] = jnp.zeros_like(left)

    @pl.when(spot == spaces - 1)
    def _():
        right[...] = jnp.zeros_like(right)

    peers = sum(there.astype(jnp.int32) for there, _target in partners)
    pl.semaphore_wait(barrier, peers)

    def z_copy(f):
        return pltpu.make_async_remote_copy(
            out_ref.at[f], own.at[f], z_send.at[f], z_recv.at[f],
            device_id=to_next, device_id_type=MESH,
        )

    def l_copy(f):
        return pltpu.make_async_remote_copy(
            own.at[f], right.at[f], l_send.at[f], l_recv.at[f],
            device_id=to_left, device_id_type=MESH,
        )

    def r_copy(f):
        return pltpu.make_async_remote_copy(
            own.at[f], left.at[f], r_send.at[f], r_recv.at[f],
            device_id=to_right, device_id_type=MESH,
        )

    def start_halo(f):
        @pl.when(has_left)
        def _():
            l_copy(f).start()

        @pl.when(has_right)
        def _():
            r_copy(f).start()

    def forward(f):
        @pl.when(has_prev)
        def _():
            z_copy(f).wait_recv()

        start_halo(f)

    def taps(v):
        grid = (v.shape[0] // cols, cols, channels)
        size = v.shape[0] - 2 * cols
        column = lax.broadcasted_iota(jnp.int32, grid, 1)
        before = pltpu.roll(v, 1, 0).reshape(grid)
        after = pltpu.roll(v, v.shape[0] - 1, 0).reshape(grid)
        shifted = (
            jnp.where(column == 0, 0.0, before).reshape(v.shape),
            v,
            jnp.where(column == cols - 1, 0.0, after).reshape(v.shape),
        )
        pieces = []
        for c in (1, 0, 2):
            even = shifted[c].astype(jnp.bfloat16)
            odd = shifted[c][cols:cols + size].astype(jnp.bfloat16)
            pieces += [even[:size], odd, even[2 * cols:]]
        return jnp.concatenate(pieces, -1)

    def conv(vs, stage, first):
        cache = caches[stage]
        wide = jnp.float32
        size = vs[0].shape[0] - 2 * cols
        if first:
            for c in w_copies(stage, 0):
                c.wait()
        lhs = jnp.concatenate([taps(v) for v in vs], 0)
        kernels = jnp.concatenate([ws[h, stage] for h in range(halves)], -1)
        rhs = jnp.concatenate(
            [kernels[(3 * r + c) * channels:(3 * r + c + 1) * channels] for c in (1, 0, 2) for r in range(3)], 0
        )
        now = jnp.dot(lhs, rhs, preferred_element_type=wide).astype(jnp.bfloat16)
        nows = [now[g * size:(g + 1) * size] for g in range(len(vs))]
        if first:
            for c in w_copies(stage, 1):
                c.wait()
            line = [nows[0], nows[0]] + nows
        else:
            line = [cache[0].astype(jnp.bfloat16), cache[1].astype(jnp.bfloat16)] + nows
        cache[0] = line[-2].astype(wide)
        cache[1] = line[-1].astype(wide)
        lhs = jnp.concatenate(
            [jnp.concatenate(line[g:g + 3], -1) for g in range(len(vs))], 0
        )
        kernels = jnp.concatenate([wt[h, stage] for h in range(halves)], -1)
        mixed = jnp.dot(lhs, kernels, preferred_element_type=wide)
        return [mixed[g * size:(g + 1) * size] for g in range(len(vs))]

    deep = depth_ref[0] > 1

    forward(0)

    def tick(f, first):
        @pl.when(f + 1 < ticks)
        def _():
            forward(f + 1)

        @pl.when(has_left)
        def _():
            r_copy(f).wait_recv()

        @pl.when(has_right)
        def _():
            l_copy(f).wait_recv()

        xs = []
        for g in range(group):
            span = slice(g * cells, (g + 1) * cells)
            xs.append(jnp.concatenate([left[f, span], own[f, span], right[f, span]], 0).astype(jnp.float32))
        bs = [edge_rows(silu(q), 3 * cols, has_left, has_right) for q in conv([silu(x) for x in xs], 0, first)]
        qs = conv(bs, 1, first)
        x1s = [(x[2 * cols:-2 * cols] + q).astype(jnp.bfloat16).astype(jnp.float32) for x, q in zip(xs, qs)]
        x1s = [edge_rows(x1, 2 * cols, has_left, has_right) for x1 in x1s]

        bs = [edge_rows(silu(q), cols, has_left, has_right) for q in conv([silu(x) for x in x1s], 2, first)]
        qs = conv(bs, 3, first)
        for g in range(group):
            mid = x1s[g][2 * cols:-2 * cols]
            out_ref[f, g * cells:(g + 1) * cells] = jnp.where(deep, mid + qs[g], mid).astype(jnp.bfloat16)

        @pl.when(has_next)
        def _():
            z_copy(f).start()

    tick(0, True)

    def later(f, carry):
        tick(f, False)
        return carry

    lax.fori_loop(1, ticks, later, 0)

    def drain(f, carry):
        @pl.when(has_next)
        def _():
            z_copy(f).wait_send()

        @pl.when(has_left)
        def _():
            l_copy(f).wait_send()

        @pl.when(has_right)
        def _():
            r_copy(f).wait_send()

        return carry

    lax.fori_loop(0, ticks, drain, 0)


def per_device(segments, spaces, video, spatial_weight, temporal_weight, section_blocks):
    micro, frames, rows, cols, channels = video.shape
    steps = micro * frames // GROUP
    cells = GROUP * rows * cols
    spatial_set = spatial_weight.reshape(4, 9 * channels, channels)
    temporal_set = temporal_weight.reshape(4, 3 * channels, channels)
    bf16 = jnp.bfloat16
    sizes = [(3 * rows - 2 * i) * cols for i in range(5)]
    dma = pltpu.SemaphoreType.DMA
    out = pl.pallas_call(
        functools.partial(kernel, segments, spaces, rows, cols),
        out_shape=jax.ShapeDtypeStruct((steps, cells, channels), bf16),
        in_specs=[
            pl.BlockSpec(memory_space=pltpu.SMEM),
            pl.BlockSpec(memory_space=pltpu.VMEM),
            pl.BlockSpec(memory_space=pl.ANY),
            pl.BlockSpec(memory_space=pl.ANY),
        ],
        out_specs=pl.BlockSpec(memory_space=pltpu.VMEM),
        scratch_shapes=[
            pltpu.VMEM((steps, cells, channels), bf16),
            pltpu.VMEM((steps, cells, channels), bf16),
            pltpu.VMEM((steps, cells, channels), bf16),
            pltpu.VMEM((channels // 128, 4, 9 * channels, 128), bf16),
            pltpu.VMEM((channels // 128, 4, 3 * channels, 128), bf16),
            [pltpu.VMEM((2, sizes[i + 1], channels), jnp.float32) for i in range(4)],
            dma((8 * channels // 128,)),
            dma((steps,)), dma((steps,)), dma((steps,)),
            dma((steps,)), dma((steps,)), dma((steps,)),
        ],
        compiler_params=pltpu.CompilerParams(
            collective_id=0, has_side_effects=True, vmem_limit_bytes=60 * 2**20
        ),
        name="sections",
    )(section_blocks, video.reshape(steps, cells, channels), spatial_set, temporal_set)
    return out.reshape(1, micro, frames, rows, cols, channels)


def solution(mesh):
    return jax.shard_map(
        functools.partial(per_device, mesh.shape["segment"], mesh.shape["space"]),
        mesh=mesh,
        in_specs=(
            P(None, None, "space", None, None),
            P("segment", None, None, None, None),
            P("segment", None, None, None, None),
            P("segment"),
        ),
        out_specs=P("segment", None, None, "space", None, None),
        check_vma=False,
    )
```

```python
import functools

import jax
import jax.numpy as jnp
from jax import lax
from jax.experimental import pallas as pl
from jax.experimental.pallas import tpu as pltpu
from jax.sharding import PartitionSpec as P

MESH = pl.DeviceIdType.MESH
GROUP = 1


def silu(v):
    half = 0.5 * v
    return half + half * jnp.tanh(half)


def edge_rows(v, width, low_ok, high_ok):
    low = jnp.where(low_ok, v[:width], 0.0)
    high = jnp.where(high_ok, v[-width:], 0.0)
    return jnp.concatenate([low, v[width:-width], high], 0)


def kernel(
    segments, spaces, rows, cols,
    depth_ref, video_ref, ws_hbm, wt_hbm, out_ref,
    own, left, right, ws, wt, caches,
    v_sem, w_sem, z_send, z_recv, l_send, l_recv, r_send, r_recv,
):
    ticks = video_ref.shape[0]
    cells = rows * cols
    group = video_ref.shape[1] // cells
    channels = video_ref.shape[2]
    halves = channels // 128
    place = lax.axis_index("segment")
    spot = lax.axis_index("space")
    has_left = spot > 0
    has_right = spot < spaces - 1
    has_prev = place > 0
    has_next = place < segments - 1

    def w_copies(i, which):
        source, target = ((ws_hbm, ws), (wt_hbm, wt))[which]
        return [
            pltpu.make_async_copy(
                source.at[i, :, pl.ds(128 * h, 128)], target.at[h, i], w_sem.at[(2 * i + which) * halves + h]
            )
            for h in range(halves)
        ]

    to_next = {"segment": place + 1}
    to_prev = {"segment": place - 1}
    to_left = {"space": spot - 1}
    to_right = {"space": spot + 1}
    partners = ((has_prev, to_prev), (has_next, to_next), (has_left, to_left), (has_right, to_right))

    barrier = pltpu.get_barrier_semaphore()
    for there, target in partners:
        @pl.when(there)
        def _():
            pl.semaphore_signal(barrier, inc=1, device_id=target, device_id_type=MESH)

    @pl.when(place == 0)
    def _():
        fetch = pltpu.make_async_copy(video_ref, own, v_sem)
        fetch.start()
        fetch.wait()

    for i in range(4):
        for c in w_copies(i, 0) + w_copies(i, 1):
            c.start()

    @pl.when(spot == 0)
    def _():
        left[...] = jnp.zeros_like(left)

    @pl.when(spot == spaces - 1)
    def _():
        right[...] = jnp.zeros_like(right)

    peers = sum(there.astype(jnp.int32) for there, _target in partners)
    pl.semaphore_wait(barrier, peers)

    def z_copy(f):
        return pltpu.make_async_remote_copy(
            out_ref.at[f], own.at[f], z_send.at[f], z_recv.at[f],
            device_id=to_next, device_id_type=MESH,
        )

    def l_copy(f):
        return pltpu.make_async_remote_copy(
            own.at[f], right.at[f], l_send.at[f], l_recv.at[f],
            device_id=to_left, device_id_type=MESH,
        )

    def r_copy(f):
        return pltpu.make_async_remote_copy(
            own.at[f], left.at[f], r_send.at[f], r_recv.at[f],
            device_id=to_right, device_id_type=MESH,
        )

    def start_halo(f):
        @pl.when(has_left)
        def _():
            l_copy(f).start()

        @pl.when(has_right)
        def _():
            r_copy(f).start()

    def forward(f):
        @pl.when(has_prev)
        def _():
            z_copy(f).wait_recv()

        start_halo(f)

    def taps(v):
        grid = (v.shape[0] // cols, cols, channels)
        size = v.shape[0] - 2 * cols
        column = lax.broadcasted_iota(jnp.int32, grid, 1)
        before = pltpu.roll(v, 1, 0).reshape(grid)
        after = pltpu.roll(v, v.shape[0] - 1, 0).reshape(grid)
        shifted = (
            jnp.where(column == 0, 0.0, before).reshape(v.shape),
            v,
            jnp.where(column == cols - 1, 0.0, after).reshape(v.shape),
        )
        pieces = []
        for c in (1, 0, 2):
            even = shifted[c].astype(jnp.bfloat16)
            odd = shifted[c][cols:cols + size].astype(jnp.bfloat16)
            pieces += [even[:size], odd, even[2 * cols:]]
        return jnp.concatenate(pieces, -1)

    def conv(vs, stage, first):
        cache = caches[stage]
        wide = jnp.float32
        size = vs[0].shape[0] - 2 * cols
        if first:
            for c in w_copies(stage, 0):
                c.wait()
        early = not first and len(vs) == 1
        if not first:
            temporal = jnp.concatenate([wt[h, stage] for h in range(halves)], -1)
        if early:
            newer = cache[1]
            past = jnp.dot(
                jnp.concatenate([cache[0], newer], -1).astype(jnp.bfloat16), temporal[:2 * channels],
                preferred_element_type=wide,
            )
        lhs = jnp.concatenate([taps(v) for v in vs], 0)
        kernels = jnp.concatenate([ws[h, stage] for h in range(halves)], -1)
        rhs = jnp.concatenate(
            [kernels[(3 * r + c) * channels:(3 * r + c + 1) * channels] for c in (1, 0, 2) for r in range(3)], 0
        )
        now = jnp.dot(lhs, rhs, preferred_element_type=wide).astype(jnp.bfloat16)
        if early:
            cache[0] = newer
            cache[1] = now.astype(wide)
            return [past + jnp.dot(now, temporal[2 * channels:], preferred_element_type=wide)]
        nows = [now[g * size:(g + 1) * size] for g in range(len(vs))]
        if first:
            for c in w_copies(stage, 1):
                c.wait()
            temporal = jnp.concatenate([wt[h, stage] for h in range(halves)], -1)
            line = [nows[0], nows[0]] + nows
        else:
            line = [cache[0].astype(jnp.bfloat16), cache[1].astype(jnp.bfloat16)] + nows
        cache[0] = line[-2].astype(wide)
        cache[1] = line[-1].astype(wide)
        lhs = jnp.concatenate(
            [jnp.concatenate(line[g:g + 3], -1) for g in range(len(vs))], 0
        )
        mixed = jnp.dot(lhs, temporal, preferred_element_type=wide)
        return [mixed[g * size:(g + 1) * size] for g in range(len(vs))]

    deep = depth_ref[0] > 1

    forward(0)

    def tick(f, first):
        @pl.when(f + 1 < ticks)
        def _():
            forward(f + 1)

        @pl.when(has_left)
        def _():
            r_copy(f).wait_recv()

        @pl.when(has_right)
        def _():
            l_copy(f).wait_recv()

        xs = []
        for g in range(group):
            span = slice(g * cells, (g + 1) * cells)
            xs.append(jnp.concatenate([left[f, span], own[f, span], right[f, span]], 0).astype(jnp.float32))
        bs = [edge_rows(silu(q), 3 * cols, has_left, has_right) for q in conv([silu(x) for x in xs], 0, first)]
        qs = conv(bs, 1, first)
        x1s = [(x[2 * cols:-2 * cols] + q).astype(jnp.bfloat16).astype(jnp.float32) for x, q in zip(xs, qs)]
        x1s = [edge_rows(x1, 2 * cols, has_left, has_right) for x1 in x1s]

        bs = [edge_rows(silu(q), cols, has_left, has_right) for q in conv([silu(x) for x in x1s], 2, first)]
        qs = conv(bs, 3, first)
        for g in range(group):
            mid = x1s[g][2 * cols:-2 * cols]
            out_ref[f, g * cells:(g + 1) * cells] = jnp.where(deep, mid + qs[g], mid).astype(jnp.bfloat16)

        @pl.when(has_next)
        def _():
            z_copy(f).start()

    tick(0, True)

    def later(f, carry):
        tick(f, False)
        return carry

    lax.fori_loop(1, ticks, later, 0)

    def drain(f, carry):
        @pl.when(has_next)
        def _():
            z_copy(f).wait_send()

        @pl.when(has_left)
        def _():
            l_copy(f).wait_send()

        @pl.when(has_right)
        def _():
            r_copy(f).wait_send()

        return carry

    lax.fori_loop(0, ticks, drain, 0)


def per_device(segments, spaces, video, spatial_weight, temporal_weight, section_blocks):
    micro, frames, rows, cols, channels = video.shape
    steps = micro * frames // GROUP
    cells = GROUP * rows * cols
    spatial_set = spatial_weight.reshape(4, 9 * channels, channels)
    temporal_set = temporal_weight.reshape(4, 3 * channels, channels)
    bf16 = jnp.bfloat16
    sizes = [(3 * rows - 2 * i) * cols for i in range(5)]
    dma = pltpu.SemaphoreType.DMA
    out = pl.pallas_call(
        functools.partial(kernel, segments, spaces, rows, cols),
        out_shape=jax.ShapeDtypeStruct((steps, cells, channels), bf16),
        in_specs=[
            pl.BlockSpec(memory_space=pltpu.SMEM),
            pl.BlockSpec(memory_space=pltpu.HBM),
            pl.BlockSpec(memory_space=pltpu.HBM),
            pl.BlockSpec(memory_space=pltpu.HBM),
        ],
        out_specs=pl.BlockSpec(memory_space=pltpu.VMEM),
        scratch_shapes=[
            pltpu.VMEM((steps, cells, channels), bf16),
            pltpu.VMEM((steps, cells, channels), bf16),
            pltpu.VMEM((steps, cells, channels), bf16),
            pltpu.VMEM((channels // 128, 4, 9 * channels, 128), bf16),
            pltpu.VMEM((channels // 128, 4, 3 * channels, 128), bf16),
            [pltpu.VMEM((2, sizes[i + 1], channels), jnp.float32) for i in range(4)],
            dma,
            dma((8 * channels // 128,)),
            dma((steps,)), dma((steps,)), dma((steps,)),
            dma((steps,)), dma((steps,)), dma((steps,)),
        ],
        compiler_params=pltpu.CompilerParams(
            collective_id=0, has_side_effects=True, vmem_limit_bytes=63 * 2**20
        ),
        name="sections",
    )(section_blocks, video.reshape(steps, cells, channels), spatial_set, temporal_set)
    return out.reshape(1, micro, frames, rows, cols, channels)


def solution(mesh):
    return jax.shard_map(
        functools.partial(per_device, mesh.shape["segment"], mesh.shape["space"]),
        mesh=mesh,
        in_specs=(
            P(None, None, "space", None, None),
            P("segment", None, None, None, None),
            P("segment", None, None, None, None),
            P("segment"),
        ),
        out_specs=P("segment", None, None, "space", None, None),
        check_vma=False,
    )
```

```python
import functools

import jax
import jax.numpy as jnp
from jax import lax
from jax.experimental import pallas as pl
from jax.experimental.pallas import tpu as pltpu
from jax.sharding import PartitionSpec as P

MESH = pl.DeviceIdType.MESH
GROUP = 1


def silu(v):
    half = 0.5 * v
    return half + half * jnp.tanh(half)


def edge_rows(v, width, low_ok, high_ok):
    low = jnp.where(low_ok, v[:width], 0.0)
    high = jnp.where(high_ok, v[-width:], 0.0)
    return jnp.concatenate([low, v[width:-width], high], 0)


def kernel(
    segments, spaces, rows, cols,
    depth_ref, video_ref, ws_hbm, wt_hbm, out_ref,
    own, left, right, ws, wt, caches,
    w_sem, z_send, z_recv, l_send, l_recv, r_send, r_recv,
):
    ticks = video_ref.shape[0]
    cells = rows * cols
    group = video_ref.shape[1] // cells
    channels = video_ref.shape[2]
    halves = channels // 128
    place = lax.axis_index("segment")
    spot = lax.axis_index("space")
    has_left = spot > 0
    has_right = spot < spaces - 1
    has_prev = place > 0
    has_next = place < segments - 1

    def w_copies(i, which):
        source, target = ((ws_hbm, ws), (wt_hbm, wt))[which]
        return [
            pltpu.make_async_copy(
                source.at[i, :, pl.ds(128 * h, 128)], target.at[h, i], w_sem.at[(2 * i + which) * halves + h]
            )
            for h in range(halves)
        ]

    for i in range(4):
        for c in w_copies(i, 0) + w_copies(i, 1):
            c.start()

    to_next = {"segment": place + 1}
    to_prev = {"segment": place - 1}
    to_left = {"space": spot - 1}
    to_right = {"space": spot + 1}
    partners = ((has_prev, to_prev), (has_next, to_next), (has_left, to_left), (has_right, to_right))

    barrier = pltpu.get_barrier_semaphore()
    for there, target in partners:
        @pl.when(there)
        def _():
            pl.semaphore_signal(barrier, inc=1, device_id=target, device_id_type=MESH)

    @pl.when(place == 0)
    def _():
        own[...] = video_ref[...]

    @pl.when(spot == 0)
    def _():
        left[...] = jnp.zeros_like(left)

    @pl.when(spot == spaces - 1)
    def _():
        right[...] = jnp.zeros_like(right)

    peers = sum(there.astype(jnp.int32) for there, _target in partners)
    pl.semaphore_wait(barrier, peers)

    def z_copy(f):
        return pltpu.make_async_remote_copy(
            out_ref.at[f], own.at[f], z_send.at[f], z_recv.at[f],
            device_id=to_next, device_id_type=MESH,
        )

    def l_copy(f):
        return pltpu.make_async_remote_copy(
            own.at[f], right.at[f], l_send.at[f], l_recv.at[f],
            device_id=to_left, device_id_type=MESH,
        )

    def r_copy(f):
        return pltpu.make_async_remote_copy(
            own.at[f], left.at[f], r_send.at[f], r_recv.at[f],
            device_id=to_right, device_id_type=MESH,
        )

    def start_halo(f):
        @pl.when(has_left)
        def _():
            l_copy(f).start()

        @pl.when(has_right)
        def _():
            r_copy(f).start()

    def forward(f):
        @pl.when(has_prev)
        def _():
            z_copy(f).wait_recv()

        start_halo(f)

    def taps(v):
        count = v.shape[0] // cols
        size = v.shape[0] - 2 * cols
        last = cols - 8
        sublane = lax.broadcasted_iota(jnp.int32, (count, 8, channels), 1)
        before = pltpu.roll(v, 1, 0).reshape(count, cols, channels)
        after = pltpu.roll(v, v.shape[0] - 1, 0).reshape(count, cols, channels)
        shifted = (
            jnp.concatenate([jnp.where(sublane == 0, 0.0, before[:, :8]), before[:, 8:]], 1).reshape(v.shape),
            v,
            jnp.concatenate([after[:, :last], jnp.where(sublane == 7, 0.0, after[:, last:])], 1).reshape(v.shape),
        )
        pieces = []
        for c in (1, 0, 2):
            even = shifted[c].astype(jnp.bfloat16)
            odd = shifted[c][cols:cols + size].astype(jnp.bfloat16)
            pieces += [even[:size], odd, even[2 * cols:]]
        return jnp.concatenate(pieces, -1)

    def conv(vs, stage, first):
        cache = caches[stage]
        wide = jnp.float32
        size = vs[0].shape[0] - 2 * cols
        if first:
            for c in w_copies(stage, 0):
                c.wait()
        lhs = jnp.concatenate([taps(v) for v in vs], 0)
        kernels = jnp.concatenate([ws[h, stage] for h in range(halves)], -1)
        rhs = jnp.concatenate(
            [kernels[(3 * r + c) * channels:(3 * r + c + 1) * channels] for c in (1, 0, 2) for r in range(3)], 0
        )
        now = jnp.dot(lhs, rhs, preferred_element_type=wide).astype(jnp.bfloat16)
        nows = [now[g * size:(g + 1) * size] for g in range(len(vs))]
        if first:
            for c in w_copies(stage, 1):
                c.wait()
            line = [nows[0], nows[0]] + nows
        else:
            line = [jnp.concatenate([cache[i, h] for h in range(halves)], -1) for i in range(2)] + nows
        for i in range(2):
            for h in range(halves):
                cache[i, h] = line[i - 2][:, 128 * h:128 * (h + 1)]
        lhs = jnp.concatenate(
            [jnp.concatenate(line[g:g + 3], -1) for g in range(len(vs))], 0
        )
        kernels = jnp.concatenate([wt[h, stage] for h in range(halves)], -1)
        mixed = jnp.dot(lhs, kernels, preferred_element_type=wide)
        return [mixed[g * size:(g + 1) * size] for g in range(len(vs))]

    deep = depth_ref[0] > 1

    forward(0)

    def tick(f, first):
        @pl.when(f + 1 < ticks)
        def _():
            forward(f + 1)

        @pl.when(has_left)
        def _():
            r_copy(f).wait_recv()

        @pl.when(has_right)
        def _():
            l_copy(f).wait_recv()

        xs = []
        for g in range(group):
            span = slice(g * cells, (g + 1) * cells)
            xs.append(jnp.concatenate([left[f, span], own[f, span], right[f, span]], 0).astype(jnp.float32))
        bs = [edge_rows(silu(q), 3 * cols, has_left, has_right) for q in conv([silu(x) for x in xs], 0, first)]
        qs = conv(bs, 1, first)
        x1s = [(x[2 * cols:-2 * cols] + q).astype(jnp.bfloat16).astype(jnp.float32) for x, q in zip(xs, qs)]
        x1s = [edge_rows(x1, 2 * cols, has_left, has_right) for x1 in x1s]

        bs = [edge_rows(silu(q), cols, has_left, has_right) for q in conv([silu(x) for x in x1s], 2, first)]
        qs = conv(bs, 3, first)
        for g in range(group):
            mid = x1s[g][2 * cols:-2 * cols]
            out_ref[f, g * cells:(g + 1) * cells] = jnp.where(deep, mid + qs[g], mid).astype(jnp.bfloat16)

        @pl.when(has_next)
        def _():
            z_copy(f).start()

    tick(0, True)

    def later(f, carry):
        tick(f, False)
        return carry

    lax.fori_loop(1, ticks, later, 0)

    def drain(f, carry):
        @pl.when(has_next)
        def _():
            z_copy(f).wait_send()

        @pl.when(has_left)
        def _():
            l_copy(f).wait_send()

        @pl.when(has_right)
        def _():
            r_copy(f).wait_send()

        return carry

    lax.fori_loop(0, ticks, drain, 0)


def per_device(segments, spaces, video, spatial_weight, temporal_weight, section_blocks):
    micro, frames, rows, cols, channels = video.shape
    steps = micro * frames // GROUP
    cells = GROUP * rows * cols
    spatial_set = spatial_weight.reshape(4, 9 * channels, channels)
    temporal_set = temporal_weight.reshape(4, 3 * channels, channels)
    bf16 = jnp.bfloat16
    sizes = [(3 * rows - 2 * i) * cols for i in range(5)]
    dma = pltpu.SemaphoreType.DMA
    out = pl.pallas_call(
        functools.partial(kernel, segments, spaces, rows, cols),
        out_shape=jax.ShapeDtypeStruct((steps, cells, channels), bf16),
        in_specs=[
            pl.BlockSpec(memory_space=pltpu.SMEM),
            pl.BlockSpec(memory_space=pltpu.VMEM),
            pl.BlockSpec(memory_space=pl.ANY),
            pl.BlockSpec(memory_space=pl.ANY),
        ],
        out_specs=pl.BlockSpec(memory_space=pltpu.VMEM),
        scratch_shapes=[
            pltpu.VMEM((steps, cells, channels), bf16),
            pltpu.VMEM((steps, cells, channels), bf16),
            pltpu.VMEM((steps, cells, channels), bf16),
            pltpu.VMEM((channels // 128, 4, 9 * channels, 128), bf16),
            pltpu.VMEM((channels // 128, 4, 3 * channels, 128), bf16),
            [pltpu.VMEM((2, channels // 128, sizes[i + 1], 128), bf16) for i in range(4)],
            dma((8 * channels // 128,)),
            dma((steps,)), dma((steps,)), dma((steps,)),
            dma((steps,)), dma((steps,)), dma((steps,)),
        ],
        compiler_params=pltpu.CompilerParams(
            collective_id=0, has_side_effects=True, vmem_limit_bytes=60 * 2**20
        ),
        name="sections",
    )(section_blocks, video.reshape(steps, cells, channels), spatial_set, temporal_set)
    return out.reshape(1, micro, frames, rows, cols, channels)


def solution(mesh):
    return jax.shard_map(
        functools.partial(per_device, mesh.shape["segment"], mesh.shape["space"]),
        mesh=mesh,
        in_specs=(
            P(None, None, "space", None, None),
            P("segment", None, None, None, None),
            P("segment", None, None, None, None),
            P("segment"),
        ),
        out_specs=P("segment", None, None, "space", None, None),
        check_vma=False,
    )
```

```python
import functools

import jax
import jax.numpy as jnp
from jax import lax
from jax.experimental import pallas as pl
from jax.experimental.pallas import tpu as pltpu
from jax.sharding import PartitionSpec as P

MESH = pl.DeviceIdType.MESH
GROUP = 2


def silu(v):
    half = 0.5 * v
    return half + half * jnp.tanh(half)


def edge_rows(v, width, low_ok, high_ok):
    low = jnp.where(low_ok, v[:width], 0.0)
    high = jnp.where(high_ok, v[-width:], 0.0)
    return jnp.concatenate([low, v[width:-width], high], 0)


def kernel(
    segments, spaces, rows, cols,
    depth_ref, video_ref, ws_hbm, wt_hbm, out_ref,
    own, left, right, ws, wt, caches,
    w_sem, z_send, z_recv, l_send, l_recv, r_send, r_recv,
):
    ticks = video_ref.shape[0]
    cells = rows * cols
    group = video_ref.shape[1] // cells
    channels = video_ref.shape[2]
    halves = channels // 128
    place = lax.axis_index("segment")
    spot = lax.axis_index("space")
    has_left = spot > 0
    has_right = spot < spaces - 1
    has_prev = place > 0
    has_next = place < segments - 1

    def w_copies(i, which):
        source, target = ((ws_hbm, ws), (wt_hbm, wt))[which]
        return [
            pltpu.make_async_copy(
                source.at[i, :, pl.ds(128 * h, 128)], target.at[h, i], w_sem.at[(2 * i + which) * halves + h]
            )
            for h in range(halves)
        ]

    for i in range(4):
        for c in w_copies(i, 0) + w_copies(i, 1):
            c.start()

    to_next = {"segment": place + 1}
    to_prev = {"segment": place - 1}
    to_left = {"space": spot - 1}
    to_right = {"space": spot + 1}
    partners = ((has_prev, to_prev), (has_next, to_next), (has_left, to_left), (has_right, to_right))

    barrier = pltpu.get_barrier_semaphore()
    for there, target in partners:
        @pl.when(there)
        def _():
            pl.semaphore_signal(barrier, inc=1, device_id=target, device_id_type=MESH)

    @pl.when(place == 0)
    def _():
        own[...] = video_ref[...]

    @pl.when(spot == 0)
    def _():
        left[...] = jnp.zeros_like(left)

    @pl.when(spot == spaces - 1)
    def _():
        right[...] = jnp.zeros_like(right)

    peers = sum(there.astype(jnp.int32) for there, _target in partners)
    pl.semaphore_wait(barrier, peers)

    def z_copy(f):
        return pltpu.make_async_remote_copy(
            out_ref.at[f], own.at[f], z_send.at[f], z_recv.at[f],
            device_id=to_next, device_id_type=MESH,
        )

    def l_copy(f):
        return pltpu.make_async_remote_copy(
            own.at[f], right.at[f], l_send.at[f], l_recv.at[f],
            device_id=to_left, device_id_type=MESH,
        )

    def r_copy(f):
        return pltpu.make_async_remote_copy(
            own.at[f], left.at[f], r_send.at[f], r_recv.at[f],
            device_id=to_right, device_id_type=MESH,
        )

    def start_halo(f):
        @pl.when(has_left)
        def _():
            l_copy(f).start()

        @pl.when(has_right)
        def _():
            r_copy(f).start()

    def forward(f):
        @pl.when(has_prev)
        def _():
            z_copy(f).wait_recv()

        start_halo(f)

    def taps(v):
        count = v.shape[0] // cols
        size = v.shape[0] - 2 * cols
        last = cols - 8
        sublane = lax.broadcasted_iota(jnp.int32, (count, 8, channels), 1)
        before = pltpu.roll(v, 1, 0).reshape(count, cols, channels)
        after = pltpu.roll(v, v.shape[0] - 1, 0).reshape(count, cols, channels)
        shifted = (
            jnp.concatenate([jnp.where(sublane == 0, 0.0, before[:, :8]), before[:, 8:]], 1).reshape(v.shape),
            v,
            jnp.concatenate([after[:, :last], jnp.where(sublane == 7, 0.0, after[:, last:])], 1).reshape(v.shape),
        )
        pieces = []
        for c in (1, 0, 2):
            even = shifted[c].astype(jnp.bfloat16)
            odd = shifted[c][cols:cols + size].astype(jnp.bfloat16)
            pieces += [even[:size], odd, even[2 * cols:]]
        return jnp.concatenate(pieces, -1)

    def conv(vs, stage, first):
        cache = caches[stage]
        wide = jnp.float32
        size = vs[0].shape[0] - 2 * cols
        if first:
            for c in w_copies(stage, 0):
                c.wait()
        lhs = jnp.concatenate([taps(v) for v in vs], 0)
        kernels = jnp.concatenate([ws[h, stage] for h in range(halves)], -1)
        rhs = jnp.concatenate(
            [kernels[(3 * r + c) * channels:(3 * r + c + 1) * channels] for c in (1, 0, 2) for r in range(3)], 0
        )
        now = jnp.dot(lhs, rhs, preferred_element_type=wide).astype(jnp.bfloat16)
        nows = [now[g * size:(g + 1) * size] for g in range(len(vs))]
        if first:
            for c in w_copies(stage, 1):
                c.wait()
            line = [nows[0], nows[0]] + nows
        else:
            line = [jnp.concatenate([cache[i, h] for h in range(halves)], -1) for i in range(2)] + nows
        for i in range(2):
            for h in range(halves):
                cache[i, h] = line[i - 2][:, 128 * h:128 * (h + 1)]
        lhs = jnp.concatenate(
            [jnp.concatenate(line[g:g + 3], -1) for g in range(len(vs))], 0
        )
        kernels = jnp.concatenate([wt[h, stage] for h in range(halves)], -1)
        mixed = jnp.dot(lhs, kernels, preferred_element_type=wide)
        return [mixed[g * size:(g + 1) * size] for g in range(len(vs))]

    deep = depth_ref[0] > 1

    forward(0)

    def tick(f, first):
        @pl.when(f + 1 < ticks)
        def _():
            forward(f + 1)

        @pl.when(has_left)
        def _():
            r_copy(f).wait_recv()

        @pl.when(has_right)
        def _():
            l_copy(f).wait_recv()

        xs = []
        for g in range(group):
            span = slice(g * cells, (g + 1) * cells)
            xs.append(jnp.concatenate([left[f, span], own[f, span], right[f, span]], 0).astype(jnp.float32))
        bs = [edge_rows(silu(q), 3 * cols, has_left, has_right) for q in conv([silu(x) for x in xs], 0, first)]
        qs = conv(bs, 1, first)
        x1s = [(x[2 * cols:-2 * cols] + q).astype(jnp.bfloat16).astype(jnp.float32) for x, q in zip(xs, qs)]
        x1s = [edge_rows(x1, 2 * cols, has_left, has_right) for x1 in x1s]

        bs = [edge_rows(silu(q), cols, has_left, has_right) for q in conv([silu(x) for x in x1s], 2, first)]
        qs = conv(bs, 3, first)
        for g in range(group):
            mid = x1s[g][2 * cols:-2 * cols]
            out_ref[f, g * cells:(g + 1) * cells] = jnp.where(deep, mid + qs[g], mid).astype(jnp.bfloat16)

        @pl.when(has_next)
        def _():
            z_copy(f).start()

    tick(0, True)

    def later(f, carry):
        tick(f, False)
        return carry

    lax.fori_loop(1, ticks, later, 0)

    def drain(f, carry):
        @pl.when(has_next)
        def _():
            z_copy(f).wait_send()

        @pl.when(has_left)
        def _():
            l_copy(f).wait_send()

        @pl.when(has_right)
        def _():
            r_copy(f).wait_send()

        return carry

    lax.fori_loop(0, ticks, drain, 0)


def per_device(segments, spaces, video, spatial_weight, temporal_weight, section_blocks):
    micro, frames, rows, cols, channels = video.shape
    steps = micro * frames // GROUP
    cells = GROUP * rows * cols
    spatial_set = spatial_weight.reshape(4, 9 * channels, channels)
    temporal_set = temporal_weight.reshape(4, 3 * channels, channels)
    bf16 = jnp.bfloat16
    sizes = [(3 * rows - 2 * i) * cols for i in range(5)]
    dma = pltpu.SemaphoreType.DMA
    out = pl.pallas_call(
        functools.partial(kernel, segments, spaces, rows, cols),
        out_shape=jax.ShapeDtypeStruct((steps, cells, channels), bf16),
        in_specs=[
            pl.BlockSpec(memory_space=pltpu.SMEM),
            pl.BlockSpec(memory_space=pltpu.VMEM),
            pl.BlockSpec(memory_space=pl.ANY),
            pl.BlockSpec(memory_space=pl.ANY),
        ],
        out_specs=pl.BlockSpec(memory_space=pltpu.VMEM),
        scratch_shapes=[
            pltpu.VMEM((steps, cells, channels), bf16),
            pltpu.VMEM((steps, cells, channels), bf16),
            pltpu.VMEM((steps, cells, channels), bf16),
            pltpu.VMEM((channels // 128, 4, 9 * channels, 128), bf16),
            pltpu.VMEM((channels // 128, 4, 3 * channels, 128), bf16),
            [pltpu.VMEM((2, channels // 128, sizes[i + 1], 128), bf16) for i in range(4)],
            dma((8 * channels // 128,)),
            dma((steps,)), dma((steps,)), dma((steps,)),
            dma((steps,)), dma((steps,)), dma((steps,)),
        ],
        compiler_params=pltpu.CompilerParams(
            collective_id=0, has_side_effects=True, vmem_limit_bytes=60 * 2**20
        ),
        name="sections",
    )(section_blocks, video.reshape(steps, cells, channels), spatial_set, temporal_set)
    return out.reshape(1, micro, frames, rows, cols, channels)


def solution(mesh):
    return jax.shard_map(
        functools.partial(per_device, mesh.shape["segment"], mesh.shape["space"]),
        mesh=mesh,
        in_specs=(
            P(None, None, "space", None, None),
            P("segment", None, None, None, None),
            P("segment", None, None, None, None),
            P("segment"),
        ),
        out_specs=P("segment", None, None, "space", None, None),
        check_vma=False,
    )
```

```python
import functools

import jax
import jax.numpy as jnp
from jax import lax
from jax.experimental import pallas as pl
from jax.experimental.pallas import tpu as pltpu
from jax.sharding import PartitionSpec as P

MESH = pl.DeviceIdType.MESH
GROUP = 1


def silu(v):
    half = 0.5 * v
    return half + half * jnp.tanh(half)


def edge_rows(v, width, low_ok, high_ok):
    low = jnp.where(low_ok, v[:width], 0.0)
    high = jnp.where(high_ok, v[-width:], 0.0)
    return jnp.concatenate([low, v[width:-width], high], 0)


def tall_dot(lhs, rhs):
    rows = lhs.shape[0]
    cut = (rows // 2 + 15) // 16 * 16
    parts = [lhs] if rows <= 128 else [lhs[:cut], lhs[cut:]]
    return jnp.concatenate([jnp.dot(p, rhs, preferred_element_type=jnp.float32) for p in parts], 0)


def kernel(
    segments, spaces, rows, cols,
    depth_ref, video_ref, ws_hbm, wt_hbm, out_ref,
    own, left, right, ws, wt, caches,
    w_sem, z_send, z_recv, l_send, l_recv, r_send, r_recv,
):
    ticks = video_ref.shape[0]
    cells = rows * cols
    group = video_ref.shape[1] // cells
    channels = video_ref.shape[2]
    halves = channels // 128
    place = lax.axis_index("segment")
    spot = lax.axis_index("space")
    has_left = spot > 0
    has_right = spot < spaces - 1
    has_prev = place > 0
    has_next = place < segments - 1

    def w_copies(i, which):
        source, target = ((ws_hbm, ws), (wt_hbm, wt))[which]
        return [
            pltpu.make_async_copy(
                source.at[i, :, pl.ds(128 * h, 128)], target.at[h, i], w_sem.at[(2 * i + which) * halves + h]
            )
            for h in range(halves)
        ]

    for i in range(4):
        for c in w_copies(i, 0) + w_copies(i, 1):
            c.start()

    to_next = {"segment": place + 1}
    to_prev = {"segment": place - 1}
    to_left = {"space": spot - 1}
    to_right = {"space": spot + 1}
    partners = ((has_prev, to_prev), (has_next, to_next), (has_left, to_left), (has_right, to_right))

    barrier = pltpu.get_barrier_semaphore()
    for there, target in partners:
        @pl.when(there)
        def _():
            pl.semaphore_signal(barrier, inc=1, device_id=target, device_id_type=MESH)

    @pl.when(place == 0)
    def _():
        own[...] = video_ref[...]

    @pl.when(spot == 0)
    def _():
        left[...] = jnp.zeros_like(left)

    @pl.when(spot == spaces - 1)
    def _():
        right[...] = jnp.zeros_like(right)

    peers = sum(there.astype(jnp.int32) for there, _target in partners)
    pl.semaphore_wait(barrier, peers)

    def z_copy(f):
        return pltpu.make_async_remote_copy(
            out_ref.at[f], own.at[f], z_send.at[f], z_recv.at[f],
            device_id=to_next, device_id_type=MESH,
        )

    def l_copy(f):
        return pltpu.make_async_remote_copy(
            own.at[f], right.at[f], l_send.at[f], l_recv.at[f],
            device_id=to_left, device_id_type=MESH,
        )

    def r_copy(f):
        return pltpu.make_async_remote_copy(
            own.at[f], left.at[f], r_send.at[f], r_recv.at[f],
            device_id=to_right, device_id_type=MESH,
        )

    def start_halo(f):
        @pl.when(has_left)
        def _():
            l_copy(f).start()

        @pl.when(has_right)
        def _():
            r_copy(f).start()

    def forward(f):
        @pl.when(has_prev)
        def _():
            z_copy(f).wait_recv()

        start_halo(f)

    def taps(v):
        count = v.shape[0] // cols
        size = v.shape[0] - 2 * cols
        last = cols - 8
        sublane = lax.broadcasted_iota(jnp.int32, (count, 8, channels), 1)
        before = pltpu.roll(v, 1, 0).reshape(count, cols, channels)
        after = pltpu.roll(v, v.shape[0] - 1, 0).reshape(count, cols, channels)
        shifted = (
            jnp.concatenate([jnp.where(sublane == 0, 0.0, before[:, :8]), before[:, 8:]], 1).reshape(v.shape),
            v,
            jnp.concatenate([after[:, :last], jnp.where(sublane == 7, 0.0, after[:, last:])], 1).reshape(v.shape),
        )
        pieces = []
        for c in (1, 0, 2):
            even = shifted[c].astype(jnp.bfloat16)
            odd = shifted[c][cols:cols + size].astype(jnp.bfloat16)
            pieces += [even[:size], odd, even[2 * cols:]]
        return jnp.concatenate(pieces, -1)

    def conv(vs, stage, first):
        cache = caches[stage]
        size = vs[0].shape[0] - 2 * cols
        if first:
            for c in w_copies(stage, 0):
                c.wait()
        lhs = jnp.concatenate([taps(v) for v in vs], 0)
        kernels = jnp.concatenate([ws[h, stage] for h in range(halves)], -1)
        rhs = jnp.concatenate(
            [kernels[(3 * r + c) * channels:(3 * r + c + 1) * channels] for c in (1, 0, 2) for r in range(3)], 0
        )
        now = tall_dot(lhs, rhs).astype(jnp.bfloat16)
        nows = [now[g * size:(g + 1) * size] for g in range(len(vs))]
        if first:
            for c in w_copies(stage, 1):
                c.wait()
            line = [nows[0], nows[0]] + nows
        else:
            line = [jnp.concatenate([cache[i, h] for h in range(halves)], -1) for i in range(2)] + nows
        for i in range(2):
            for h in range(halves):
                cache[i, h] = line[i - 2][:, 128 * h:128 * (h + 1)]
        lhs = jnp.concatenate(
            [jnp.concatenate(line[g:g + 3], -1) for g in range(len(vs))], 0
        )
        kernels = jnp.concatenate([wt[h, stage] for h in range(halves)], -1)
        mixed = tall_dot(lhs, kernels)
        return [mixed[g * size:(g + 1) * size] for g in range(len(vs))]

    deep = depth_ref[0] > 1

    forward(0)

    def tick(f, first):
        @pl.when(f + 1 < ticks)
        def _():
            forward(f + 1)

        @pl.when(has_left)
        def _():
            r_copy(f).wait_recv()

        @pl.when(has_right)
        def _():
            l_copy(f).wait_recv()

        xs = []
        for g in range(group):
            span = slice(g * cells, (g + 1) * cells)
            xs.append(jnp.concatenate([left[f, span], own[f, span], right[f, span]], 0).astype(jnp.float32))
        bs = [edge_rows(silu(q), 3 * cols, has_left, has_right) for q in conv([silu(x) for x in xs], 0, first)]
        qs = conv(bs, 1, first)
        x1s = [(x[2 * cols:-2 * cols] + q).astype(jnp.bfloat16).astype(jnp.float32) for x, q in zip(xs, qs)]
        x1s = [edge_rows(x1, 2 * cols, has_left, has_right) for x1 in x1s]

        bs = [edge_rows(silu(q), cols, has_left, has_right) for q in conv([silu(x) for x in x1s], 2, first)]
        qs = conv(bs, 3, first)
        for g in range(group):
            mid = x1s[g][2 * cols:-2 * cols]
            out_ref[f, g * cells:(g + 1) * cells] = jnp.where(deep, mid + qs[g], mid).astype(jnp.bfloat16)

        @pl.when(has_next)
        def _():
            z_copy(f).start()

    tick(0, True)

    def later(f, carry):
        tick(f, False)
        return carry

    lax.fori_loop(1, ticks, later, 0)

    def drain(f, carry):
        @pl.when(has_next)
        def _():
            z_copy(f).wait_send()

        @pl.when(has_left)
        def _():
            l_copy(f).wait_send()

        @pl.when(has_right)
        def _():
            r_copy(f).wait_send()

        return carry

    lax.fori_loop(0, ticks, drain, 0)


def per_device(segments, spaces, video, spatial_weight, temporal_weight, section_blocks):
    micro, frames, rows, cols, channels = video.shape
    steps = micro * frames // GROUP
    cells = GROUP * rows * cols
    spatial_set = spatial_weight.reshape(4, 9 * channels, channels)
    temporal_set = temporal_weight.reshape(4, 3 * channels, channels)
    bf16 = jnp.bfloat16
    sizes = [(3 * rows - 2 * i) * cols for i in range(5)]
    dma = pltpu.SemaphoreType.DMA
    out = pl.pallas_call(
        functools.partial(kernel, segments, spaces, rows, cols),
        out_shape=jax.ShapeDtypeStruct((steps, cells, channels), bf16),
        in_specs=[
            pl.BlockSpec(memory_space=pltpu.SMEM),
            pl.BlockSpec(memory_space=pltpu.VMEM),
            pl.BlockSpec(memory_space=pl.ANY),
            pl.BlockSpec(memory_space=pl.ANY),
        ],
        out_specs=pl.BlockSpec(memory_space=pltpu.VMEM),
        scratch_shapes=[
            pltpu.VMEM((steps, cells, channels), bf16),
            pltpu.VMEM((steps, cells, channels), bf16),
            pltpu.VMEM((steps, cells, channels), bf16),
            pltpu.VMEM((channels // 128, 4, 9 * channels, 128), bf16),
            pltpu.VMEM((channels // 128, 4, 3 * channels, 128), bf16),
            [pltpu.VMEM((2, channels // 128, sizes[i + 1], 128), bf16) for i in range(4)],
            dma((8 * channels // 128,)),
            dma((steps,)), dma((steps,)), dma((steps,)),
            dma((steps,)), dma((steps,)), dma((steps,)),
        ],
        compiler_params=pltpu.CompilerParams(
            collective_id=0, has_side_effects=True, vmem_limit_bytes=60 * 2**20
        ),
        name="sections",
    )(section_blocks, video.reshape(steps, cells, channels), spatial_set, temporal_set)
    return out.reshape(1, micro, frames, rows, cols, channels)


def solution(mesh):
    return jax.shard_map(
        functools.partial(per_device, mesh.shape["segment"], mesh.shape["space"]),
        mesh=mesh,
        in_specs=(
            P(None, None, "space", None, None),
            P("segment", None, None, None, None),
            P("segment", None, None, None, None),
            P("segment"),
        ),
        out_specs=P("segment", None, None, "space", None, None),
        check_vma=False,
    )
```
